32 devices in a mesh: ex: 2 (over x), tp: 4 (over y, core), blk: 4 (over z).
Axes of the slice: x: 2, y: 2, z: 4, core: 2. Of those that a mesh axis runs over, the one named last changes fastest.
Arguments:
- gradients: bfloat16 [512, 8192], P('ex', 'tp'), may hold values from -6 to 6
- selection: int32 [256], P('ex'), may hold values from 0 to 255, as said below
- seed_value: int32 [1], replicated, may hold values from 0 to 999999999
- ridge_value: float32 [1], replicated, may hold values from 0.3 to 3
Outputs:
- panel_out: float32 [2048, 512], P(('ex', 'blk'))
- trailing: float32 [2048, 2048], P(('ex', 'blk'), 'tp')
The draws below stay inside these ranges and needn't reach their ends.
Inputs may be any that keep to these rules, and one draw needn't show every extreme that they name: `selection`: within each aligned block of 128 entries the values are distinct, and 0 and 255 occur in every block.
All inputs are finite; a program needn't handle non-finite values.
Results may differ from the reference program's by a relative error of at most 0.0046.
Values may be sent and summed in bfloat16 or wider, within the bound.
No kernel may reach another device: no remote copies, remote signals or barrier semaphores. Data moves between devices by JAX's collectives and lax.ppermute only.
A program may use at most 64 MiB of HBM per device.

```python
import math
import jax
import jax.numpy as jnp
from jax import lax

PANEL = 512
K = 2048
E_DEV = 128
GL = 2048
POOL_DEV = 256
POOLS = 512
EXAMPLES = 256
GDIM = 8192


def draw_selection(key, part):
    block_count = EXAMPLES // E_DEV

    def one_block(block_key):
        first_key, second_key = jax.random.split(block_key)
        middle = jax.random.permutation(first_key, POOL_DEV - 2).astype(jnp.int32) + 1
        picked = jnp.concatenate([jnp.zeros((1,), jnp.int32), jnp.full((1,), POOL_DEV - 1, jnp.int32), middle[:E_DEV - 2]])
        return jax.random.permutation(second_key, picked)
    keys = jax.random.split(jax.random.fold_in(key, 7), block_count)
    return jax.vmap(one_block)(keys).reshape(-1).astype(jnp.int32)


def shard_levels(key, shape, shards, smallest, largest):
    gain = 1.0
    for position, parts in shards:
        steps = jax.random.uniform(jax.random.fold_in(jax.random.fold_in(key, 6), position), (parts,), jnp.float32, smallest / len(shards), largest / len(shards))
        gain = gain * jnp.repeat(jnp.exp(steps), shape[position] // parts).reshape((-1,) + (1,) * (len(shape) - 1 - position))
    return gain


def normal_values(stream_key, extent, spread, bound, cuts=(), held_as=jnp.bfloat16):
    entries = spread * jax.random.normal(stream_key, extent, jnp.float32)
    if cuts:
        entries = entries * shard_levels(stream_key, extent, cuts, -0.22, 0.18)
    return jnp.clip(entries, -bound, bound).astype(held_as)


def setup_inputs(seed: int = 0) -> dict:
    splits = jax.random.split(jax.random.key(seed), 5)
    gradients = normal_values(splits[0], (POOLS, GDIM), 1.0, 6.0, ((0, 2), (1, 4)))
    selection = draw_selection(jax.random.fold_in(splits[4], 71), 0)
    seed_value = jax.random.randint(splits[2], (1,), 0, 1000000000).astype(jnp.int32)
    ridge_value = jnp.clip(jnp.exp(jax.random.uniform(splits[3], (1,), jnp.float32, math.log(0.3), math.log(3.0))), 0.3, 3.0)
    return {"gradients": gradients, "selection": selection, "seed_value": seed_value, "ridge_value": ridge_value}


def scramble(hashed, amount):
    return hashed ^ lax.shift_right_logical(hashed, jnp.full_like(hashed, amount))

def sign_block(seed_word, coordinates, features):
    hashed = coordinates[:, None] * jnp.int32(-1640531535) + features[None, :] * jnp.int32(668265263) + seed_word
    hashed = scramble(hashed, 16) * jnp.int32(-2048144789)
    hashed = scramble(hashed, 13) * jnp.int32(-1028477387)
    hashed = scramble(hashed, 16)
    bit_value = lax.shift_right_logical(hashed, jnp.full_like(hashed, 7)) & jnp.int32(1)
    return jnp.int32(1) - jnp.int32(2) * bit_value

def reference(gradients, selection, seed_value, ridge_value):
    row_ids = selection + jnp.arange(EXAMPLES, dtype=jnp.int32) // E_DEV * POOL_DEV
    chosen = gradients[row_ids].astype(jnp.float32)
    stride = min(512, GL)
    feature_ids = jnp.arange(K, dtype=jnp.int32)

    def accumulate(running, index):
        coordinates = index * stride + jnp.arange(stride, dtype=jnp.int32)
        sign_values = sign_block(seed_value[0], coordinates, feature_ids).astype(jnp.float32)
        slab = lax.dynamic_slice_in_dim(chosen, index * stride, stride, 1)
        return (running + jnp.dot(slab, sign_values, precision=lax.Precision.HIGHEST), None)
    projected, _ = lax.scan(accumulate, jnp.zeros((EXAMPLES, K), jnp.float32), jnp.arange(GDIM // stride, dtype=jnp.int32))
    scaling = 1.0 / math.sqrt(GDIM)
    features = (projected * scaling).astype(jnp.bfloat16).astype(jnp.float32)
    gram = jnp.dot(features.T, features, precision=lax.Precision.HIGHEST) / float(EXAMPLES)
    diagonal_ids = jnp.arange(K, dtype=jnp.int32)
    gram = gram.at[diagonal_ids, diagonal_ids].add(ridge_value[0])
    factor = jnp.linalg.cholesky(gram[:PANEL, :PANEL])
    lifted = jax.scipy.linalg.solve_triangular(factor, gram[:PANEL, :], lower=True)
    panel_out = lifted.T
    trailing = gram - jnp.dot(panel_out, lifted, precision=lax.Precision.HIGHEST)
    return (panel_out, trailing)
```

```python
import functools
import math

import jax
import jax.numpy as jnp
from jax import lax
from jax.experimental import pallas as pl
from jax.experimental.pallas import tpu as pltpu
from jax.sharding import PartitionSpec as P

PANEL = 512
HALF = 256
LEAF = 32
BLOCK = 128
HIGHEST = lax.Precision.HIGHEST
VMEM = pl.BlockSpec(memory_space=pltpu.VMEM)
SMEM = pl.BlockSpec(memory_space=pltpu.SMEM)


def scramble(hashed, amount):
    return hashed ^ lax.shift_right_logical(hashed, jnp.full_like(hashed, amount))


def sign_block(seed_word, coordinates, features):
    hashed = (
        coordinates[:, None] * jnp.int32(-1640531535)
        + features[None, :] * jnp.int32(668265263)
        + seed_word
    )
    hashed = scramble(hashed, 16) * jnp.int32(-2048144789)
    hashed = scramble(hashed, 13) * jnp.int32(-1028477387)
    hashed = scramble(hashed, 16)
    bit_value = lax.shift_right_logical(hashed, jnp.full_like(hashed, 7)) & jnp.int32(1)
    return jnp.int32(1) - jnp.int32(2) * bit_value


def project(chosen, seed_word, first_coordinate, feature_ids):
    coord_dev = chosen.shape[1]
    stride = min(512, coord_dev)
    projected = jnp.zeros((chosen.shape[0], feature_ids.shape[0]), jnp.float32)
    for start in range(0, coord_dev, stride):
        coordinates = first_coordinate + start + jnp.arange(stride, dtype=jnp.int32)
        sign_values = sign_block(seed_word, coordinates, feature_ids).astype(jnp.bfloat16)
        projected = projected + jnp.dot(
            chosen[:, start : start + stride], sign_values, preferred_element_type=jnp.float32
        )
    return projected


def tdot(left, right, precision=HIGHEST):
    return lax.dot_general(
        left, right, (((0,), (0,)), ((), ())), precision=precision, preferred_element_type=jnp.float32
    )


def row_of(value, row):
    return jnp.broadcast_to(value[row : row + 1, :], value.shape)


def factor_leaf(rows_u, rows_z, offset):
    groups = len(rows_u)
    sub = lax.broadcasted_iota(jnp.int32, (8, BLOCK), 0)
    columns = [
        [
            None if v < c // 8 else jnp.broadcast_to(rows_u[v][:, offset + c : offset + c + 1], (8, BLOCK))
            for v in range(groups)
        ]
        for c in range(8 * groups)
    ]
    rows_u, rows_z = list(rows_u), list(rows_z)
    pivots = [jnp.ones((8, BLOCK), jnp.float32) for _ in range(groups)]
    for j in range(8 * groups):
        g, s = divmod(j, 8)
        column = columns[j]
        pivot = row_of(column[g], s)
        pivots[g] = jnp.where(sub == s, pivot, pivots[g])
        inverse = 1.0 / pivot
        factors = {v: column[v] * inverse for v in range(g, groups)}
        factors[g] = jnp.where(sub > s, factors[g], 0.0)
        for c in range(j + 1, 8 * groups):
            weight = row_of(column[c // 8], c % 8)
            for v in range(c // 8, groups):
                columns[c][v] = columns[c][v] - factors[v] * weight
        row_u, row_z = row_of(rows_u[g], s), row_of(rows_z[g], s)
        for v in range(g, groups):
            rows_u[v] = rows_u[v] - factors[v] * row_u
            rows_z[v] = rows_z[v] - factors[v] * row_z
    scales = [lax.rsqrt(pivot) for pivot in pivots]
    return (
        jnp.concatenate([row * scale for row, scale in zip(rows_u, scales)], axis=0),
        jnp.concatenate([row * scale for row, scale in zip(rows_z, scales)], axis=0),
    )


def identity_mask(shape):
    return lax.broadcasted_iota(jnp.int32, shape, 0) == lax.broadcasted_iota(jnp.int32, shape, 1)


def factor_block(block):
    rest = jnp.concatenate([block, identity_mask(block.shape).astype(jnp.float32)], axis=1)
    done = []
    for leaf in range(BLOCK // LEAF):
        rows = [rest[8 * v : 8 * v + 8] for v in range(LEAF // 8)]
        upper, inverse = factor_leaf(
            [row[:, :BLOCK] for row in rows], [row[:, BLOCK:] for row in rows], LEAF * leaf
        )
        done.append(inverse)
        if leaf + 1 < BLOCK // LEAF:
            update = tdot(upper, jnp.concatenate([upper, inverse], axis=1))
            rest = rest[LEAF:] - update[LEAF * (leaf + 1) :]
    return jnp.concatenate(done, axis=0)


def cholesky_kernel(ridge_ref, phi_ref, upper_ref, lifted_ref, gram_ref):
    examples, width = phi_ref.shape
    phi = phi_ref[...]
    gram_ref[...] = tdot(phi, phi, None) / float(examples) + jnp.where(
        identity_mask((width, width)), ridge_ref[0], 0.0
    )
    lifted_ref[...] = phi.astype(jnp.float32).T
    for low in range(0, width, BLOCK):
        high = low + BLOCK
        inverse = factor_block(gram_ref[low:high, low:high])
        upper = jnp.dot(
            inverse, gram_ref[low:high, low:], precision=HIGHEST, preferred_element_type=jnp.float32
        )
        lifted = jnp.dot(
            inverse, lifted_ref[low:high, :], precision=HIGHEST, preferred_element_type=jnp.float32
        )
        keep = lax.broadcasted_iota(jnp.int32, upper.shape, 0) <= lax.broadcasted_iota(
            jnp.int32, upper.shape, 1
        )
        upper_ref[low:high, low:] = jnp.where(keep, upper, 0.0)
        if low > 0:
            upper_ref[low:high, :low] = jnp.zeros((BLOCK, low), jnp.float32)
        lifted_ref[low:high, :] = lifted
        if high < width:
            rest = upper[:, BLOCK:]
            gram_ref[high:, high:] = gram_ref[high:, high:] - tdot(rest, rest)
            lifted_ref[high:, :] = lifted_ref[high:, :] - tdot(rest, lifted)


def cholesky_panel(ridge_value, phi_panel):
    examples, width = phi_panel.shape
    return pl.pallas_call(
        cholesky_kernel,
        out_shape=(
            jax.ShapeDtypeStruct((width, width), jnp.float32),
            jax.ShapeDtypeStruct((width, examples), jnp.float32),
        ),
        in_specs=[SMEM, VMEM],
        out_specs=(VMEM, VMEM),
        scratch_shapes=[pltpu.VMEM((width, width), jnp.float32)],
        compiler_params=pltpu.CompilerParams(vmem_limit_bytes=32 * 1024 * 1024),
        cost_estimate=pl.CostEstimate(flops=20_000_000_000, bytes_accessed=4_000_000, transcendentals=0),
        name="cholesky_panel",
    )(ridge_value, phi_panel)


def split_dot(left, right):
    total = None
    for _ in range(3):
        part = left.astype(jnp.bfloat16)
        left = left - part.astype(jnp.float32)
        term = jnp.dot(part, right, preferred_element_type=jnp.float32)
        total = term if total is None else total + term
    return total


def finish_kernel(place_ref, ridge_ref, upper_ref, lifted_ref, rows_ref, columns_ref, panel_ref, trailing_ref):
    examples, height = rows_ref.shape
    width = columns_ref.shape[1]
    panel = upper_ref.shape[0]
    row_start = place_ref[0]
    column_start = place_ref[1]
    rows, columns = rows_ref[...], columns_ref[...]
    lifted = lifted_ref[...]
    solved_rows = split_dot(lifted, rows) / float(examples)
    solved_columns = split_dot(lifted, columns) / float(examples)
    for start in range(0, panel, height):
        solved_rows = jnp.where(row_start == start, upper_ref[:, start : start + height], solved_rows)
    for start in range(0, panel, width):
        solved_columns = jnp.where(column_start == start, upper_ref[:, start : start + width], solved_columns)
    panel_ref[...] = solved_rows.T
    shape = (height, width)
    diagonal = row_start + lax.broadcasted_iota(jnp.int32, shape, 0) == column_start + lax.broadcasted_iota(
        jnp.int32, shape, 1
    )
    gram = tdot(rows, columns, None) / float(examples) + jnp.where(diagonal, ridge_ref[0], 0.0)
    trailing_ref[...] = gram - tdot(solved_rows, solved_columns)


def finish(place, ridge_value, upper, lifted, phi_rows, phi_columns):
    height, width = phi_rows.shape[1], phi_columns.shape[1]
    return pl.pallas_call(
        finish_kernel,
        out_shape=(
            jax.ShapeDtypeStruct((height, upper.shape[0]), jnp.float32),
            jax.ShapeDtypeStruct((height, width), jnp.float32),
        ),
        in_specs=[SMEM, SMEM, VMEM, VMEM, VMEM, VMEM],
        out_specs=(VMEM, VMEM),
        compiler_params=pltpu.CompilerParams(vmem_limit_bytes=32 * 1024 * 1024),
        cost_estimate=pl.CostEstimate(flops=2_000_000_000, bytes_accessed=4_000_000, transcendentals=0),
        name="finish",
    )(place, ridge_value, upper, lifted, phi_rows, phi_columns)


def shifted(value, axis, step):
    count = lax.axis_size(axis)
    return lax.ppermute(value, axis, [(s, (s + step) % count) for s in range(count)])


def exchange(pieces, axis):
    count = lax.axis_size(axis)
    index = lax.axis_index(axis)
    return [pieces(index)] + [
        shifted(pieces((index + step) % count), axis, step) for step in range(1, count)
    ]


def shards(gradients, selection, seed_value, ridge_value):
    ex_count = lax.axis_size("ex")
    tp_count = lax.axis_size("tp")
    blk_count = lax.axis_size("blk")
    ex_index, tp_index, blk_index = (lax.axis_index(axis) for axis in ("ex", "tp", "blk"))
    example_rows_dev = selection.shape[0]
    coord_dev = gradients.shape[1]
    chunk = example_rows_dev // tp_count
    column_width = HALF * ex_count * blk_count // tp_count
    scaling = 1.0 / math.sqrt(coord_dev * tp_count)
    chosen = gradients[selection]
    first_coordinate = tp_index * coord_dev

    def reduced(partial):
        def piece(target):
            return lax.dynamic_slice_in_dim(partial, target * chunk, chunk, 0)

        parts = exchange(piece, "tp")
        return (functools.reduce(jnp.add, parts) * scaling).astype(jnp.bfloat16)

    panel_ids = jnp.arange(PANEL, dtype=jnp.int32)
    phi_panel = reduced(project(chosen, seed_value[0], first_coordinate, panel_ids))
    phi_panel = jnp.stack(exchange(lambda target: phi_panel, "ex"))
    phi_panel = jnp.stack(exchange(lambda target: phi_panel, "tp"), axis=1).reshape(-1, PANEL)

    upper, lifted = cholesky_panel(ridge_value, phi_panel)

    feature_ids = (
        (jnp.arange(ex_count, dtype=jnp.int32)[:, None] * blk_count + blk_index) * HALF
        + jnp.arange(HALF, dtype=jnp.int32)[None, :]
    ).reshape(-1)
    phi_own = reduced(project(chosen, seed_value[0], first_coordinate, feature_ids))
    back = exchange(lambda target: phi_own.reshape(chunk, ex_count, 1, HALF), "blk")
    steps = (blk_index - jnp.arange(blk_count)) % blk_count
    phi_all = jnp.take(jnp.concatenate(back, axis=2), steps, axis=2).reshape(chunk, -1)

    def both(target):
        columns = lax.dynamic_slice_in_dim(phi_all, target * column_width, column_width, 1)
        return jnp.concatenate([columns, phi_own], axis=1)

    phi_both = jnp.concatenate(exchange(both, "tp"), axis=0)

    def half_of(target):
        rows = lax.dynamic_slice_in_dim(phi_both, column_width + target * HALF, HALF, 1)
        return jnp.concatenate([phi_both[:, :column_width], rows], axis=1)

    phi_both = jnp.concatenate(exchange(half_of, "ex"), axis=0)
    phi_columns, phi_rows = phi_both[:, :column_width], phi_both[:, column_width:]
    place = jnp.stack([(ex_index * blk_count + blk_index) * HALF, tp_index * column_width]).astype(jnp.int32)
    return finish(place, ridge_value, upper, lifted, phi_rows, phi_columns)


def solution(mesh):
    in_specs = (P("ex", "tp"), P("ex"), P(), P())
    out_specs = (P(("ex", "blk"), None), P(("ex", "blk"), "tp"))
    return jax.shard_map(shards, mesh=mesh, in_specs=in_specs, out_specs=out_specs, check_vma=False)
```

```python
import math

import jax
import jax.numpy as jnp
from jax import lax
from jax.experimental import pallas as pl
from jax.experimental.pallas import tpu as pltpu
from jax.sharding import PartitionSpec as P

PANEL = 512
HALF = 256
STRIPE = 32
SUB = 16
BLOCK = 128
DEPTH = 256
HIGHEST = lax.Precision.HIGHEST
VMEM = pl.BlockSpec(memory_space=pltpu.VMEM)
SMEM = pl.BlockSpec(memory_space=pltpu.SMEM)


def scramble(hashed, amount):
    return hashed ^ lax.shift_right_logical(hashed, jnp.full_like(hashed, amount))


def sign_block(seed_word, coordinates, features):
    hashed = (
        coordinates[:, None] * jnp.int32(-1640531535)
        + features[None, :] * jnp.int32(668265263)
        + seed_word
    )
    hashed = scramble(hashed, 16) * jnp.int32(-2048144789)
    hashed = scramble(hashed, 13) * jnp.int32(-1028477387)
    hashed = scramble(hashed, 16)
    bit_value = lax.shift_right_logical(hashed, jnp.full_like(hashed, 7)) & jnp.int32(1)
    return jnp.int32(1) - jnp.int32(2) * bit_value


def project(chosen, seed_word, first_coordinate, feature_ids):
    coord_dev = chosen.shape[1]
    stride = min(512, coord_dev)
    projected = jnp.zeros((chosen.shape[0], feature_ids.shape[0]), jnp.float32)
    for start in range(0, coord_dev, stride):
        coordinates = first_coordinate + start + jnp.arange(stride, dtype=jnp.int32)
        sign_values = sign_block(seed_word, coordinates, feature_ids).astype(jnp.bfloat16)
        projected = projected + jnp.dot(
            chosen[:, start : start + stride], sign_values, preferred_element_type=jnp.float32
        )
    return projected


def tdot(left, right, precision=HIGHEST):
    return lax.dot_general(
        left, right, (((0,), (0,)), ((), ())), precision=precision, preferred_element_type=jnp.float32
    )


def row_of(value, row):
    return jnp.broadcast_to(value[row : row + 1, :], value.shape)


def join(parts, axis):
    return parts[0] if len(parts) == 1 else jnp.concatenate(parts, axis)


def factor_stripe(rows_u, rows_z, offset):
    groups = len(rows_u)
    sub = lax.broadcasted_iota(jnp.int32, (8, BLOCK), 0)
    rows_u, rows_z = list(rows_u), list(rows_z)
    pivots = [jnp.ones((8, BLOCK), jnp.float32) for _ in range(groups)]
    for base in range(0, 8 * groups, SUB):
        columns = {
            c: {
                v: jnp.broadcast_to(rows_u[v][:, offset + c : offset + c + 1], (8, BLOCK))
                for v in range(c // 8, groups)
            }
            for c in range(base, base + SUB)
        }
        pivot = row_of(columns[base][base // 8], 0)
        for j in range(base, base + SUB):
            g, s = divmod(j, 8)
            column = columns[j]
            inverse = 1.0 / pivot
            pivots[g] = jnp.where(sub == s, pivot, pivots[g])
            if j + 1 < base + SUB:
                n, r = divmod(j + 1, 8)
                weight = row_of(column[n], r)
                following = columns[j + 1]
                pivot = row_of(following[n], r) - (weight * weight) * inverse
                for v in range(n, groups):
                    following[v] = following[v] - (column[v] * weight) * inverse
            factors = {v: column[v] * inverse for v in range(g, groups)}
            for c in range(j + 2, base + SUB):
                weight = row_of(column[c // 8], c % 8)
                for v in range(c // 8, groups):
                    columns[c][v] = columns[c][v] - factors[v] * weight
            factors[g] = jnp.where(sub > s, factors[g], 0.0)
            row_u, row_z = row_of(rows_u[g], s), row_of(rows_z[g], s)
            for v in range(g + (s == 7), groups):
                rows_u[v] = rows_u[v] - factors[v] * row_u
                rows_z[v] = rows_z[v] - factors[v] * row_z
    scales = [lax.rsqrt(pivot) for pivot in pivots]
    return (
        [row * scale for row, scale in zip(rows_u, scales)],
        [row * scale for row, scale in zip(rows_z, scales)],
    )


def thirds(value):
    high = value.astype(jnp.bfloat16)
    rest = value - high.astype(jnp.float32)
    middle = rest.astype(jnp.bfloat16)
    return high, middle, (rest - middle.astype(jnp.float32)).astype(jnp.bfloat16)


def exact_dot(left, right, transposed=False):
    axis = 0 if transposed else 1
    left_parts, right_parts = thirds(left), thirds(right)
    terms = ((0, 0), (0, 1), (1, 0), (0, 2), (2, 0), (1, 1))
    count = max(1, min(len(terms), DEPTH // left.shape[axis]))
    total = None
    for start in range(0, len(terms), count):
        some = terms[start : start + count]
        term = lax.dot_general(
            join([left_parts[i] for i, _ in some], axis),
            join([right_parts[j] for _, j in some], 0),
            (((axis,), (0,)), ((), ())),
            preferred_element_type=jnp.float32,
        )
        total = term if total is None else total + term
    return total


def identity_mask(shape):
    return lax.broadcasted_iota(jnp.int32, shape, 0) == lax.broadcasted_iota(jnp.int32, shape, 1)


def factor_block(block):
    unit = identity_mask(block.shape).astype(jnp.float32)
    rows_u = [block[8 * v : 8 * v + 8] for v in range(BLOCK // 8)]
    rows_z = [unit[8 * v : 8 * v + 8] for v in range(BLOCK // 8)]
    groups = STRIPE // 8
    done = []
    for end in range(STRIPE, BLOCK + 1, STRIPE):
        upper, inverse = factor_stripe(rows_u[:groups], rows_z[:groups], end - STRIPE)
        done += inverse
        if end < BLOCK:
            upper, inverse = jnp.concatenate(upper, axis=0), jnp.concatenate(inverse, axis=0)
            update = exact_dot(upper, jnp.concatenate([upper, inverse], axis=1), True)[end:]
            rows_u = [row - update[8 * v : 8 * v + 8, :BLOCK] for v, row in enumerate(rows_u[groups:])]
            rows_z = [row - update[8 * v : 8 * v + 8, BLOCK:] for v, row in enumerate(rows_z[groups:])]
    return jnp.concatenate(done, axis=0)


def cholesky_kernel(ridge_ref, phi_ref, upper_ref, lifted_ref, gram_ref):
    examples, width = phi_ref.shape
    phi = phi_ref[...]
    gram_ref[...] = tdot(phi, phi, None) / float(examples) + jnp.where(
        identity_mask((width, width)), ridge_ref[0], 0.0
    )
    lifted_ref[...] = phi.astype(jnp.float32).T
    square = (BLOCK, BLOCK)
    keep = lax.broadcasted_iota(jnp.int32, square, 0) <= lax.broadcasted_iota(jnp.int32, square, 1)
    block = gram_ref[:BLOCK, :BLOCK]
    for low in range(0, width, BLOCK):
        high = low + BLOCK
        after = high + BLOCK
        current = block
        inverse = factor_block(current)
        if high < width:
            beside = exact_dot(inverse, gram_ref[low:high, high:after])
            block = gram_ref[high:after, high:after] - exact_dot(beside, beside, True)
            upper_ref[low:high, high:after] = beside
        upper_ref[low:high, low:high] = jnp.where(keep, exact_dot(inverse, current), 0.0)
        if low > 0:
            upper_ref[low:high, :low] = jnp.zeros((BLOCK, low), jnp.float32)
        lifted = exact_dot(inverse, lifted_ref[low:high, :])
        lifted_ref[low:high, :] = lifted
        if high < width:
            lifted_ref[high:after, :] = lifted_ref[high:after, :] - exact_dot(beside, lifted, True)
        if after < width:
            beyond = exact_dot(inverse, gram_ref[low:high, after:])
            upper_ref[low:high, after:] = beyond
            gram_ref[high:after, after:] = gram_ref[high:after, after:] - exact_dot(beside, beyond, True)
            gram_ref[after:, after:] = gram_ref[after:, after:] - exact_dot(beyond, beyond, True)
            lifted_ref[after:, :] = lifted_ref[after:, :] - exact_dot(beyond, lifted, True)


def cholesky_panel(ridge_value, phi_panel):
    examples, width = phi_panel.shape
    return pl.pallas_call(
        cholesky_kernel,
        out_shape=(
            jax.ShapeDtypeStruct((width, width), jnp.float32),
            jax.ShapeDtypeStruct((width, examples), jnp.float32),
        ),
        in_specs=[SMEM, VMEM],
        out_specs=(VMEM, VMEM),
        scratch_shapes=[pltpu.VMEM((width, width), jnp.float32)],
        compiler_params=pltpu.CompilerParams(vmem_limit_bytes=32 * 1024 * 1024),
        cost_estimate=pl.CostEstimate(flops=20_000_000_000, bytes_accessed=4_000_000, transcendentals=0),
        name="cholesky_panel",
    )(ridge_value, phi_panel)


def split_dot(left, right):
    total = None
    for _ in range(3):
        part = left.astype(jnp.bfloat16)
        left = left - part.astype(jnp.float32)
        term = jnp.dot(part, right, preferred_element_type=jnp.float32)
        total = term if total is None else total + term
    return total


def finish_kernel(place_ref, ridge_ref, upper_ref, lifted_ref, rows_ref, columns_ref, panel_ref, trailing_ref):
    examples, height = rows_ref.shape
    width = columns_ref.shape[1]
    panel = upper_ref.shape[0]
    row_start = place_ref[0]
    column_start = place_ref[1]
    rows, columns = rows_ref[...], columns_ref[...]
    lifted = lifted_ref[...]
    solved_rows = split_dot(lifted, rows) / float(examples)
    solved_columns = split_dot(lifted, columns) / float(examples)
    for start in range(0, panel, height):
        solved_rows = jnp.where(row_start == start, upper_ref[:, start : start + height], solved_rows)
    for start in range(0, panel, width):
        solved_columns = jnp.where(column_start == start, upper_ref[:, start : start + width], solved_columns)
    panel_ref[...] = solved_rows.T
    shape = (height, width)
    diagonal = row_start + lax.broadcasted_iota(jnp.int32, shape, 0) == column_start + lax.broadcasted_iota(
        jnp.int32, shape, 1
    )
    gram = tdot(rows, columns, None) / float(examples) + jnp.where(diagonal, ridge_ref[0], 0.0)
    trailing_ref[...] = gram - tdot(solved_rows, solved_columns)


def finish(place, ridge_value, upper, lifted, phi_rows, phi_columns):
    height, width = phi_rows.shape[1], phi_columns.shape[1]
    return pl.pallas_call(
        finish_kernel,
        out_shape=(
            jax.ShapeDtypeStruct((height, upper.shape[0]), jnp.float32),
            jax.ShapeDtypeStruct((height, width), jnp.float32),
        ),
        in_specs=[SMEM, SMEM, VMEM, VMEM, VMEM, VMEM],
        out_specs=(VMEM, VMEM),
        compiler_params=pltpu.CompilerParams(vmem_limit_bytes=32 * 1024 * 1024),
        cost_estimate=pl.CostEstimate(flops=2_000_000_000, bytes_accessed=4_000_000, transcendentals=0),
        name="finish",
    )(place, ridge_value, upper, lifted, phi_rows, phi_columns)


def swapped(value, axis, bit):
    return lax.ppermute(value, axis, [(s, s ^ bit) for s in range(lax.axis_size(axis))])


def shards(gradients, selection, seed_value, ridge_value):
    ex_count = lax.axis_size("ex")
    tp_count = lax.axis_size("tp")
    blk_count = lax.axis_size("blk")
    ex_index, tp_index, blk_index = (lax.axis_index(axis) for axis in ("ex", "tp", "blk"))
    coord_dev = gradients.shape[1]
    column_width = HALF * ex_count * blk_count // tp_count
    scaling = 1.0 / math.sqrt(coord_dev * tp_count)
    chosen = gradients[selection]

    feature_ids = jnp.concatenate(
        [
            jnp.arange(PANEL, dtype=jnp.int32),
            (
                (jnp.arange(ex_count, dtype=jnp.int32)[:, None] * blk_count + blk_index) * HALF
                + jnp.arange(HALF, dtype=jnp.int32)[None, :]
            ).reshape(-1),
        ]
    )
    partial = project(chosen, seed_value[0], tp_index * coord_dev, feature_ids)

    half = partial.shape[0] // 2
    low_bit = tp_index % 2
    total = lax.dynamic_slice_in_dim(partial, low_bit * half, half, 0) + swapped(
        lax.dynamic_slice_in_dim(partial, (1 - low_bit) * half, half, 0), "tp", 1
    )
    bit = 2
    while bit < tp_count:
        total = total + swapped(total, "tp", bit)
        bit *= 2
    phi = (total * scaling).astype(jnp.bfloat16)

    column_ex = tp_index * column_width // (blk_count * HALF)

    def group(which):
        return lax.dynamic_slice_in_dim(phi, PANEL + which * HALF, HALF, 1)

    def piece(target):
        return jnp.concatenate([phi[:, :PANEL], group(target), group(column_ex)], axis=1)

    gathered = [piece(ex_index)]
    for step in range(1, ex_count):
        gathered.append(swapped(piece(ex_index ^ step), "ex", step))
    gathered = jnp.concatenate(gathered, axis=0)
    gathered = jnp.concatenate([gathered, swapped(gathered, "tp", 1)], axis=0)
    phi_panel, phi_rows, share = (
        gathered[:, :PANEL],
        gathered[:, PANEL : PANEL + HALF],
        gathered[:, PANEL + HALF :],
    )

    groups = column_width // HALF

    def first_source(tp):
        return tp * groups % blk_count

    columns = [jnp.zeros_like(share)] * groups
    source = first_source(tp_index)
    for step in range(blk_count):
        if step == 0:
            came = share
        else:
            pairs = []
            for tp in range(tp_count):
                for blk in range(blk_count):
                    if first_source(tp) <= blk < first_source(tp) + groups:
                        pairs.append((tp * blk_count + blk, tp * blk_count + (blk ^ step)))
            came = lax.ppermute(share, ("tp", "blk"), pairs)
        for which in range(groups):
            columns[which] = jnp.where(blk_index ^ step == source + which, came, columns[which])
    phi_columns = jnp.concatenate(columns, axis=1)

    upper, lifted = cholesky_panel(ridge_value, phi_panel)
    place = jnp.stack([(ex_index * blk_count + blk_index) * HALF, tp_index * column_width]).astype(jnp.int32)
    return finish(place, ridge_value, upper, lifted, phi_rows, phi_columns)


def solution(mesh):
    in_specs = (P("ex", "tp"), P("ex"), P(), P())
    out_specs = (P(("ex", "blk"), None), P(("ex", "blk"), "tp"))
    return jax.shard_map(shards, mesh=mesh, in_specs=in_specs, out_specs=out_specs, check_vma=False)
```

```python
import functools
import math

import jax
import jax.numpy as jnp
import numpy as np
from jax import lax
from jax.experimental import pallas as pl
from jax.experimental.pallas import tpu as pltpu
from jax.sharding import PartitionSpec as P

PANEL = 512
HALF = 256
STRIPE = 32
SUB = 16
BLOCK = 128
DEPTH = 256
SEGMENT = 128
SECOND_BY_8 = int(np.array(-1028477387 << 8 & 0xFFFFFFFF, np.uint32).astype(np.int32))
SECOND_BY_24 = int(np.array(-1028477387 << 24 & 0xFFFFFFFF, np.uint32).astype(np.int32))
VMEM = pl.BlockSpec(memory_space=pltpu.VMEM)
SMEM = pl.BlockSpec(memory_space=pltpu.SMEM)
ANYWHERE = pl.BlockSpec(memory_space=pl.ANY)


def call(kernel, out_shape, in_specs, microseconds, name, scratch=(), vmem=16):
    shapes = [jax.ShapeDtypeStruct(shape, dtype) for shape, dtype in out_shape]
    return pl.pallas_call(
        kernel,
        out_shape=shapes,
        in_specs=in_specs,
        out_specs=[VMEM] * len(shapes),
        scratch_shapes=list(scratch),
        compiler_params=pltpu.CompilerParams(vmem_limit_bytes=vmem * 1024 * 1024),
        cost_estimate=pl.CostEstimate(
            flops=int(microseconds * 1_100_000_000), bytes_accessed=1_000_000, transcendentals=0
        ),
        name=name,
    )


def join(parts, axis):
    return parts[0] if len(parts) == 1 else jnp.concatenate(parts, axis)


def shifted(value, amount):
    return lax.shift_right_logical(value, jnp.full_like(value, amount))


def sign_tile(seed_word, coordinate, feature, shape):
    rows = (lax.broadcasted_iota(jnp.int32, (shape[0], 1), 0) + coordinate) * jnp.int32(-1640531535)
    columns = (lax.broadcasted_iota(jnp.int32, (1, shape[1]), 1) + feature) * jnp.int32(668265263) + seed_word
    hashed = rows + columns
    hashed = (hashed ^ shifted(hashed, 16)) * jnp.int32(-2048144789)
    hashed = hashed ^ shifted(hashed, 13)
    decided = (hashed * jnp.int32(SECOND_BY_8)) ^ (hashed * jnp.int32(SECOND_BY_24))
    return jnp.where(decided < 0, -1.0, 1.0).astype(jnp.bfloat16)


def segment_signs(words_ref, feature, width, index):
    return sign_tile(words_ref[0], words_ref[1] + index * SEGMENT, feature, (SEGMENT, width))


def project_step(words_ref, chosen_ref, feature, width, index, total):
    start = pl.multiple_of(index * SEGMENT, SEGMENT)
    signs = segment_signs(words_ref, feature, width, index)
    return total + jnp.dot(chosen_ref[:, pl.ds(start, SEGMENT)], signs, preferred_element_type=jnp.float32)


def project_tile(words_ref, chosen_ref, feature, width, unroll):
    rows, coordinates = chosen_ref.shape
    step = functools.partial(project_step, words_ref, chosen_ref, feature, width)
    zero = jnp.zeros((rows, width), jnp.float32)
    return lax.fori_loop(0, coordinates // SEGMENT, step, zero, unroll=unroll)


def panel_signs_kernel(words_ref, signs_ref):
    coordinates, width = signs_ref.shape
    for step in range(coordinates // SEGMENT):
        signs_ref[step * SEGMENT : (step + 1) * SEGMENT, :] = segment_signs(words_ref, 0, width, step)


def panel_signs(words, coordinates):
    return call(
        panel_signs_kernel, [((coordinates, PANEL), jnp.bfloat16)], [SMEM], 2, "panel_signs"
    )(words)[0]


def panel_part_kernel(words_ref, selection_ref, pool_ref, signs_ref, mine_ref, theirs_ref, chosen_ref):
    half = mine_ref.shape[0]
    shape = (pool_ref.shape[0], chosen_ref.shape[0])
    picked = jnp.where(lax.broadcasted_iota(jnp.int32, shape, 0) == selection_ref[...], 1.0, 0.0)
    chosen = tdot(picked.astype(jnp.bfloat16), pool_ref[...]).astype(jnp.bfloat16)
    chosen_ref[...] = chosen
    total = jnp.dot(chosen, signs_ref[...], preferred_element_type=jnp.float32)
    even = words_ref[2] == 0
    mine_ref[...] = jnp.where(even, total[:half], total[half:])
    theirs_ref[...] = jnp.where(even, total[half:], total[:half])


def panel_part(words, selection, pool):
    rows, coordinates = selection.shape[0], pool.shape[1]
    return call(
        panel_part_kernel,
        [((rows // 2, PANEL), jnp.float32)] * 2 + [((rows, coordinates), jnp.bfloat16)],
        [SMEM, VMEM, VMEM, VMEM],
        1,
        "panel_part",
    )(words, selection[None, :], pool, panel_signs(words, coordinates))


def blocks_part_kernel(blocks, words_ref, chosen_ref, _, *part_refs):
    width = part_refs[0].shape[1]
    for block, part_ref in zip(blocks, part_refs):
        part_ref[...] = project_tile(words_ref, chosen_ref, block * width, width, len(blocks) <= 2)


def blocks_part(words, chosen, blocks, width, after):
    return call(
        functools.partial(blocks_part_kernel, blocks),
        [((chosen.shape[0], width), jnp.float32)] * len(blocks),
        [SMEM, VMEM, ANYWHERE],
        2 * len(blocks),
        "blocks_part",
        vmem=32 if len(blocks) > 2 else 16,
    )(words, chosen, after)


def other_parts_kernel(tp_count, blk_count, words_ref, chosen_ref, _, *refs):
    *first_refs, mine_ref, theirs_ref = refs
    rows = chosen_ref.shape[0]
    half = rows // 2
    width = first_refs[0].shape[1]
    groups = width // HALF
    row_lanes = tp_count * groups // blk_count * HALF
    even = words_ref[2] == 0
    for ref in (mine_ref, theirs_ref):
        ref[:, : row_lanes + 2 * width] = jnp.zeros((half, row_lanes + 2 * width), jnp.float32)

    def place(ref, lane, part):
        ref[:, lane : lane + width] = part[:half]
        ref[:, lane + width : lane + 2 * width] = part[half:]

    for block in range(1, tp_count):
        lane = row_lanes + block // 2 * 2 * width
        if block <= len(first_refs):
            part = first_refs[block - 1][...]
        else:
            part = project_tile(words_ref, chosen_ref, block * width, width, tp_count <= 4)
        own = words_ref[2] == block % 2
        pl.when(own)(functools.partial(place, mine_ref, lane, part))
        pl.when(jnp.logical_not(own))(functools.partial(place, theirs_ref, lane, part))
        for which in range(groups):
            group = block * groups + which

            @pl.when(words_ref[3] == group % blk_count)
            def _(part=part[:, which * HALF : (which + 1) * HALF], lane=group // blk_count * HALF):
                mine_ref[:, lane : lane + HALF] = jnp.where(even, part[:half], part[half:])
                theirs_ref[:, lane : lane + HALF] = jnp.where(even, part[half:], part[:half])


def other_parts(words, chosen, first, tp_count, blk_count, after):
    rows, width = first[0].shape
    lanes = tp_count * (width // HALF) // blk_count * HALF + tp_count // 2 * 2 * width
    return call(
        functools.partial(other_parts_kernel, tp_count, blk_count),
        [((rows // 2, lanes), jnp.float32)] * 2,
        [SMEM, VMEM, ANYWHERE] + [VMEM] * len(first),
        2 * (tp_count - 1 - len(first)),
        "other_parts",
        vmem=16 if tp_count <= 4 else 48,
    )(words, chosen, after, *first)


def halve_kernel(row_lanes, bit, words_ref, left_ref, right_ref, keep_ref, send_ref):
    upper = words_ref[4] & bit != 0
    rows = left_ref[:, :row_lanes] + right_ref[:, :row_lanes]
    columns = left_ref[:, row_lanes:] + right_ref[:, row_lanes:]
    middle = columns.shape[1] // 2
    keep_ref[:, :row_lanes] = rows
    send_ref[:, :row_lanes] = rows
    keep_ref[:, row_lanes:] = jnp.where(upper, columns[:, middle:], columns[:, :middle])
    send_ref[:, row_lanes:] = jnp.where(upper, columns[:, :middle], columns[:, middle:])


def halve(words, left, right, row_lanes, bit):
    shape = (left.shape[0], (left.shape[1] + row_lanes) // 2)
    return call(
        functools.partial(halve_kernel, row_lanes, bit),
        [(shape, jnp.float32)] * 2,
        [SMEM, VMEM, VMEM],
        0.5,
        "halve",
    )(words, left, right)


def pieces_kernel(ex_count, scaling, words_ref, left_ref, right_ref, _, *piece_refs):
    row_lanes = ex_count * HALF
    total = ((left_ref[...] + right_ref[...]) * scaling).astype(jnp.bfloat16)
    for step, ref in enumerate(piece_refs):
        target = words_ref[5] ^ step
        rows = total[:, :HALF]
        for index in range(1, ex_count):
            rows = jnp.where(target == index, total[:, index * HALF : (index + 1) * HALF], rows)
        ref[:, :HALF] = rows
        ref[:, HALF:] = total[:, row_lanes:]


def pieces(words, left, right, ex_count, scaling, after):
    shape = (left.shape[0], left.shape[1] - (ex_count - 1) * HALF)
    return call(
        functools.partial(pieces_kernel, ex_count, scaling),
        [(shape, jnp.bfloat16)] * ex_count,
        [SMEM, VMEM, VMEM, ANYWHERE],
        0.5,
        "pieces",
    )(words, left, right, after)


def tdot(left, right):
    return lax.dot_general(left, right, (((0,), (0,)), ((), ())), preferred_element_type=jnp.float32)


def row_of(value, row):
    return jnp.broadcast_to(value[row : row + 1, :], value.shape)


def factor_stripe(rows_u, rows_z, offset):
    groups = len(rows_u)
    sub = lax.broadcasted_iota(jnp.int32, (8, BLOCK), 0)
    rows_u, rows_z = list(rows_u), list(rows_z)
    pivots = [jnp.ones((8, BLOCK), jnp.float32) for _ in range(groups)]
    for base in range(0, 8 * groups, SUB):
        columns = {
            c: {
                v: jnp.broadcast_to(rows_u[v][:, offset + c : offset + c + 1], (8, BLOCK))
                for v in range(c // 8, groups)
            }
            for c in range(base, base + SUB)
        }
        pivot = row_of(columns[base][base // 8], 0)
        for j in range(base, base + SUB):
            g, s = divmod(j, 8)
            column = columns[j]
            inverse = 1.0 / pivot
            pivots[g] = jnp.where(sub == s, pivot, pivots[g])
            if j + 1 < base + SUB:
                n, r = divmod(j + 1, 8)
                weight = row_of(column[n], r)
                following = columns[j + 1]
                pivot = row_of(following[n], r) - (weight * weight) * inverse
                for v in range(n, groups):
                    following[v] = following[v] - (column[v] * weight) * inverse
            factors = {v: column[v] * inverse for v in range(g, groups)}
            for c in range(j + 2, base + SUB):
                weight = row_of(column[c // 8], c % 8)
                for v in range(c // 8, groups):
                    columns[c][v] = columns[c][v] - factors[v] * weight
            factors[g] = jnp.where(sub > s, factors[g], 0.0)
            row_u, row_z = row_of(rows_u[g], s), row_of(rows_z[g], s)
            for v in range(g + (s == 7), groups):
                rows_u[v] = rows_u[v] - factors[v] * row_u
                rows_z[v] = rows_z[v] - factors[v] * row_z
    scales = [lax.rsqrt(pivot) for pivot in pivots]
    return (
        [row * scale for row, scale in zip(rows_u, scales)],
        [row * scale for row, scale in zip(rows_z, scales)],
    )


def thirds(value):
    high = value.astype(jnp.bfloat16)
    rest = value - high.astype(jnp.float32)
    middle = rest.astype(jnp.bfloat16)
    return high, middle, (rest - middle.astype(jnp.float32)).astype(jnp.bfloat16)


def exact_dot(left, right, transposed=False):
    axis = 0 if transposed else 1
    left_parts, right_parts = thirds(left), thirds(right)
    terms = ((0, 0), (0, 1), (1, 0), (0, 2), (2, 0), (1, 1))
    count = max(1, min(len(terms), DEPTH // left.shape[axis]))
    total = None
    for start in range(0, len(terms), count):
        some = terms[start : start + count]
        term = lax.dot_general(
            join([left_parts[i] for i, _ in some], axis),
            join([right_parts[j] for _, j in some], 0),
            (((axis,), (0,)), ((), ())),
            preferred_element_type=jnp.float32,
        )
        total = term if total is None else total + term
    return total


def sum_kernel(scaling, left_ref, right_ref, _, sum_ref):
    sum_ref[...] = ((left_ref[...] + right_ref[...]) * scaling).astype(jnp.bfloat16)


def scaled_sum(left, right, scaling, after):
    return pl.pallas_call(
        functools.partial(sum_kernel, scaling),
        out_shape=jax.ShapeDtypeStruct(left.shape, jnp.bfloat16),
        in_specs=[VMEM, VMEM, ANYWHERE],
        out_specs=VMEM,
        cost_estimate=pl.CostEstimate(flops=1_000_000, bytes_accessed=1_000_000, transcendentals=0),
        name="scaled_sum",
    )(left, right, after)


def identity_mask(shape):
    return lax.broadcasted_iota(jnp.int32, shape, 0) == lax.broadcasted_iota(jnp.int32, shape, 1)


def factor_block(block):
    unit = identity_mask(block.shape).astype(jnp.float32)
    rows_u = [block[8 * v : 8 * v + 8] for v in range(BLOCK // 8)]
    rows_z = [unit[8 * v : 8 * v + 8] for v in range(BLOCK // 8)]
    groups = STRIPE // 8
    done = []
    for end in range(STRIPE, BLOCK + 1, STRIPE):
        upper, inverse = factor_stripe(rows_u[:groups], rows_z[:groups], end - STRIPE)
        done += inverse
        if end < BLOCK:
            upper, inverse = jnp.concatenate(upper, axis=0), jnp.concatenate(inverse, axis=0)
            update = exact_dot(upper, jnp.concatenate([upper, inverse], axis=1), True)[end:]
            rows_u = [row - update[8 * v : 8 * v + 8, :BLOCK] for v, row in enumerate(rows_u[groups:])]
            rows_z = [row - update[8 * v : 8 * v + 8, BLOCK:] for v, row in enumerate(rows_z[groups:])]
    return jnp.concatenate(done, axis=0)


def in_pair_order(even, refs, lanes=slice(None)):
    values = [ref[:, lanes] for ref in refs]
    count = len(values) // 2
    mine, other = join(values[:count], 0), join(values[count:], 0)
    return join([jnp.where(even, mine, other), jnp.where(even, other, mine)], 0)


def eliminate(gram, lifted, upper_ref, done_ref, gram_ref, lifted_ref):
    inverse = factor_block(gram(slice(0, BLOCK), slice(0, BLOCK)))
    square = (BLOCK, BLOCK)
    keep = lax.broadcasted_iota(jnp.int32, square, 0) <= lax.broadcasted_iota(jnp.int32, square, 1)
    upper = exact_dot(inverse, gram(slice(0, BLOCK), slice(None)))
    upper_ref[:, :BLOCK] = jnp.where(keep, upper[:, :BLOCK], 0.0)
    done = exact_dot(inverse, lifted(slice(0, BLOCK)))
    done_ref[...] = done
    if gram_ref is not None:
        rest = upper[:, BLOCK:]
        upper_ref[:, BLOCK:] = rest
        gram_ref[...] = gram(slice(BLOCK, None), slice(BLOCK, None)) - exact_dot(rest, rest, True)
        lifted_ref[...] = lifted(slice(BLOCK, None)) - exact_dot(rest, done, True)


def first_block_kernel(words_ref, ridge_ref, *refs):
    *phi_refs, upper_ref, done_ref, gram_ref, lifted_ref, whole_ref, turned_ref = refs
    phi = in_pair_order(words_ref[2] == 0, phi_refs)
    examples, width = phi.shape
    whole_ref[...] = tdot(phi, phi) * (1.0 / examples) + jnp.where(
        identity_mask((width, width)), ridge_ref[0], 0.0
    )
    turned_ref[...] = phi.astype(jnp.float32).T
    eliminate(
        lambda rows, lanes: whole_ref[rows, lanes],
        lambda rows: turned_ref[rows, :],
        upper_ref,
        done_ref,
        gram_ref,
        lifted_ref,
    )


def block_kernel(gram_in, lifted_in, upper_ref, done_ref, gram_ref=None, lifted_ref=None):
    eliminate(
        lambda rows, lanes: gram_in[rows, lanes],
        lambda rows: lifted_in[rows, :],
        upper_ref,
        done_ref,
        gram_ref,
        lifted_ref,
    )


def block_shapes(width, examples):
    rest = width - BLOCK
    shapes = [(BLOCK, width), (BLOCK, examples)]
    if rest:
        shapes += [(rest, rest), (rest, examples)]
    return [(shape, jnp.float32) for shape in shapes]


def first_block(words, ridge_value, phi):
    examples, width = sum(part.shape[0] for part in phi), phi[0].shape[1]
    return call(
        first_block_kernel,
        block_shapes(width, examples),
        [SMEM, SMEM] + [VMEM] * len(phi),
        3.5,
        "gram_first_block",
        [pltpu.VMEM((width, width), jnp.float32), pltpu.VMEM((width, examples), jnp.float32)],
    )(words, ridge_value, *phi)


def next_block(gram, lifted, microseconds):
    return call(
        block_kernel, block_shapes(gram.shape[0], lifted.shape[1]), [VMEM, VMEM], microseconds, "eliminate_block"
    )(gram, lifted)


def finish_kernel(blocks, count, words_ref, ridge_ref, *refs):
    uppers, dones = refs[:blocks], refs[blocks : 2 * blocks]
    phi_refs, piece_refs = refs[2 * blocks : 2 * blocks + count], refs[2 * blocks + count : -3]
    panel_ref, trailing_ref, solved_ref = refs[-3:]
    height, panel = panel_ref.shape
    width = trailing_ref.shape[1]
    even = words_ref[2] == 0
    row_group, column_block = words_ref[6], words_ref[4]
    phi = in_pair_order(even, phi_refs)
    examples = phi.shape[0]
    rows = in_pair_order(even, piece_refs, slice(0, height))
    for start in range(0, panel, height):
        rows = jnp.where(row_group * height == start, phi[:, start : start + height], rows)
    mine = piece_refs[: count // 2]
    columns = join(
        [ref[:, start : start + width] for start in (height, height + width) for ref in mine], 0
    )
    columns = jnp.where(column_block == 0, phi, columns)
    parts = thirds(join([ref[...] for ref in dones], 0))
    parts = join(list(parts), 1)
    scale = 1.0 / examples
    solved_ref[...] = jnp.dot(parts, join([columns] * 3, 0), preferred_element_type=jnp.float32) * scale
    panel_ref[...] = (
        lax.dot_general(
            join([rows] * 3, 0), parts, (((0,), (1,)), ((), ())), preferred_element_type=jnp.float32
        )
        * scale
    )

    @pl.when(column_block == 0)
    def _():
        for index, ref in enumerate(uppers):
            low = index * BLOCK
            if low:
                solved_ref[low : low + BLOCK, :low] = jnp.zeros((BLOCK, low), jnp.float32)
            solved_ref[low : low + BLOCK, low:] = ref[...]

    for group in range(panel // height):

        @pl.when(row_group == group)
        def _(left=group * height, right=(group + 1) * height):
            for index, ref in enumerate(uppers):
                low = index * BLOCK
                lanes = slice(low, low + BLOCK)
                for start in range(left, right, BLOCK):
                    if start < low:
                        value = jnp.zeros((BLOCK, BLOCK), jnp.float32)
                    else:
                        value = ref[:, start - low : start - low + BLOCK].T
                    panel_ref[start - left : start - left + BLOCK, lanes] = value

    shape = (height, width)
    diagonal = row_group * height + lax.broadcasted_iota(
        jnp.int32, shape, 0
    ) == column_block * width + lax.broadcasted_iota(jnp.int32, shape, 1)
    gram = tdot(rows, columns) * scale + jnp.where(diagonal, ridge_ref[0], 0.0)
    trailing_ref[...] = gram - exact_dot(panel_ref[...], solved_ref[...])


def finish(words, ridge_value, uppers, dones, phi, gathered, height, width):
    panel = uppers[0].shape[1]
    operands = [*uppers, *dones, *phi, *gathered]
    return call(
        functools.partial(finish_kernel, len(uppers), len(phi)),
        [((height, panel), jnp.float32), ((height, width), jnp.float32)],
        [SMEM, SMEM] + [VMEM] * len(operands),
        3,
        "finish",
        [pltpu.VMEM((panel, width), jnp.float32)],
        vmem=24,
    )(words, ridge_value, *operands)


def swapped(value, axis, bit):
    return lax.ppermute(value, axis, [(s, s ^ bit) for s in range(lax.axis_size(axis))])


def ex_parts(own):
    return [own[0]] + [swapped(own[step], "ex", step) for step in range(1, lax.axis_size("ex"))]


def with_pair(parts):
    return list(parts) + [swapped(part, "tp", 1) for part in parts]


def shards(gradients, selection, seed_value, ridge_value):
    ex_count = lax.axis_size("ex")
    tp_count = lax.axis_size("tp")
    blk_count = lax.axis_size("blk")
    ex_index, tp_index, blk_index = (lax.axis_index(axis) for axis in ("ex", "tp", "blk"))
    coord_dev = gradients.shape[1]
    column_width = HALF * ex_count * blk_count // tp_count
    row_lanes = ex_count * HALF
    scaling = 1.0 / math.sqrt(coord_dev * tp_count)
    words = jnp.stack(
        [
            seed_value[0],
            tp_index * coord_dev,
            tp_index % 2,
            blk_index,
            tp_index,
            ex_index,
            ex_index * blk_count + blk_index,
        ]
    ).astype(jnp.int32)

    mine, theirs, chosen = panel_part(words, selection, gradients)
    total = mine + swapped(theirs, "tp", 1)
    halves = total
    bit = 2
    while bit < tp_count:
        total = total + swapped(total, "tp", bit)
        bit *= 2
    phi = ex_parts([(total * scaling).astype(jnp.bfloat16)] * ex_count)

    first = blocks_part(words, chosen, range(1, 1 + tp_count // 2), column_width, halves)
    left, right = other_parts(words, chosen, first, tp_count, blk_count, total)
    right = swapped(right, "tp", 1)
    bit = tp_count // 2
    while bit > 1:
        left, right = halve(words, left, right, row_lanes, bit)
        right = swapped(right, "tp", bit)
        bit //= 2

    phi[1:], left = lax.optimization_barrier((phi[1:], left))
    phi = with_pair(phi)
    uppers, dones = [], []
    upper, done, *rest = first_block(words, ridge_value, phi)
    while True:
        uppers.append(upper)
        dones.append(done)
        if not rest:
            break
        upper, done, *rest = next_block(*rest, 0.3 if len(dones) < 2 else 4)
    gathered = pieces(words, left, right, ex_count, scaling, dones[len(dones) // 2 - 1])
    gathered = with_pair(ex_parts(gathered))
    return tuple(finish(words, ridge_value, uppers, dones, phi, gathered, HALF, column_width))


def solution(mesh):
    in_specs = (P("ex", "tp"), P("ex"), P(), P())
    out_specs = (P(("ex", "blk"), None), P(("ex", "blk"), "tp"))
    return jax.shard_map(shards, mesh=mesh, in_specs=in_specs, out_specs=out_specs, check_vma=False)
```

```python
import functools
import math

import jax
import jax.numpy as jnp
from jax import lax
from jax.experimental import pallas as pl
from jax.experimental.pallas import tpu as pltpu
from jax.sharding import PartitionSpec as P

PANEL = 512
HALF = 256
STRIPE = 32
SUB = 16
BLOCK = 128
DEPTH = 256
SEGMENT = 128
VMEM = pl.BlockSpec(memory_space=pltpu.VMEM)
SMEM = pl.BlockSpec(memory_space=pltpu.SMEM)
ANYWHERE = pl.BlockSpec(memory_space=pl.ANY)


def call(kernel, out_shape, in_specs, microseconds, name, scratch=(), vmem=16):
    shapes = [jax.ShapeDtypeStruct(shape, dtype) for shape, dtype in out_shape]
    return pl.pallas_call(
        kernel,
        out_shape=shapes,
        in_specs=in_specs,
        out_specs=[VMEM] * len(shapes),
        scratch_shapes=list(scratch),
        compiler_params=pltpu.CompilerParams(vmem_limit_bytes=vmem * 1024 * 1024),
        cost_estimate=pl.CostEstimate(
            flops=int(microseconds * 1_100_000_000), bytes_accessed=1_000_000, transcendentals=0
        ),
        name=name,
    )


def join(parts, axis):
    return parts[0] if len(parts) == 1 else jnp.concatenate(parts, axis)


def shifted(value, amount):
    return lax.shift_right_logical(value, jnp.full_like(value, amount))


def sign_tile(seed_word, coordinate, feature, shape):
    rows = (lax.broadcasted_iota(jnp.int32, (shape[0], 1), 0) + coordinate) * jnp.int32(-1640531535)
    columns = (lax.broadcasted_iota(jnp.int32, (1, shape[1]), 1) + feature) * jnp.int32(668265263) + seed_word
    hashed = rows + columns
    hashed = (hashed ^ shifted(hashed, 16)) * jnp.int32(-2048144789)
    hashed = (hashed ^ shifted(hashed, 13)) * jnp.int32(-1028477387)
    decided = (hashed ^ shifted(hashed, 16)).astype(jnp.int16) & jnp.int16(128)
    return jnp.where(decided == 0, jnp.bfloat16(1.0), jnp.bfloat16(-1.0))


def segment_signs(words_ref, feature, width, index):
    return sign_tile(words_ref[0], words_ref[1] + index * SEGMENT, feature, (SEGMENT, width))


def project_step(words_ref, chosen_ref, feature, width, index, total):
    start = pl.multiple_of(index * SEGMENT, SEGMENT)
    signs = segment_signs(words_ref, feature, width, index)
    return total + jnp.dot(chosen_ref[:, pl.ds(start, SEGMENT)], signs, preferred_element_type=jnp.float32)


def project_tile(words_ref, chosen_ref, feature, width, unroll):
    rows, coordinates = chosen_ref.shape
    step = functools.partial(project_step, words_ref, chosen_ref, feature, width)
    zero = jnp.zeros((rows, width), jnp.float32)
    return lax.fori_loop(0, coordinates // SEGMENT, step, zero, unroll=unroll)


def panel_signs_kernel(words_ref, signs_ref):
    coordinates, width = signs_ref.shape
    for step in range(coordinates // SEGMENT):
        signs_ref[step * SEGMENT : (step + 1) * SEGMENT, :] = segment_signs(words_ref, 0, width, step)


def panel_signs(words, coordinates):
    return call(
        panel_signs_kernel, [((coordinates, PANEL), jnp.bfloat16)], [SMEM], 2, "panel_signs"
    )(words)[0]


def panel_part_kernel(words_ref, selection_ref, pool_ref, signs_ref, mine_ref, theirs_ref, chosen_ref):
    half = mine_ref.shape[0]
    shape = (pool_ref.shape[0], chosen_ref.shape[0])
    picked = jnp.where(lax.broadcasted_iota(jnp.int32, shape, 0) == selection_ref[...], 1.0, 0.0)
    chosen = tdot(picked.astype(jnp.bfloat16), pool_ref[...]).astype(jnp.bfloat16)
    chosen_ref[...] = chosen
    total = jnp.dot(chosen, signs_ref[...], preferred_element_type=jnp.float32)
    even = words_ref[2] == 0
    mine_ref[...] = jnp.where(even, total[:half], total[half:])
    theirs_ref[...] = jnp.where(even, total[half:], total[:half])


def panel_part(words, selection, pool):
    rows, coordinates = selection.shape[0], pool.shape[1]
    return call(
        panel_part_kernel,
        [((rows // 2, PANEL), jnp.float32)] * 2 + [((rows, coordinates), jnp.bfloat16)],
        [SMEM, VMEM, VMEM, VMEM],
        1,
        "panel_part",
    )(words, selection[None, :], pool, panel_signs(words, coordinates))


def blocks_part_kernel(blocks, words_ref, chosen_ref, _, *part_refs):
    width = part_refs[0].shape[1]
    for block, part_ref in zip(blocks, part_refs):
        part_ref[...] = project_tile(words_ref, chosen_ref, block * width, width, len(blocks) <= 2)


def blocks_part(words, chosen, blocks, width, after):
    return call(
        functools.partial(blocks_part_kernel, blocks),
        [((chosen.shape[0], width), jnp.float32)] * len(blocks),
        [SMEM, VMEM, ANYWHERE],
        2 * len(blocks),
        "blocks_part",
        vmem=32 if len(blocks) > 2 else 16,
    )(words, chosen, after)


def other_parts_kernel(tp_count, blk_count, words_ref, chosen_ref, _, *refs):
    *first_refs, mine_ref, theirs_ref = refs
    rows = chosen_ref.shape[0]
    half = rows // 2
    width = first_refs[0].shape[1]
    groups = width // HALF
    row_lanes = tp_count * groups // blk_count * HALF
    even = words_ref[2] == 0
    for ref in (mine_ref, theirs_ref):
        ref[:, : row_lanes + 2 * width] = jnp.zeros((half, row_lanes + 2 * width), jnp.float32)

    def place(ref, lane, part):
        ref[:, lane : lane + width] = part[:half]
        ref[:, lane + width : lane + 2 * width] = part[half:]

    for block in range(1, tp_count):
        lane = row_lanes + block // 2 * 2 * width
        if block <= len(first_refs):
            part = first_refs[block - 1][...]
        else:
            part = project_tile(words_ref, chosen_ref, block * width, width, tp_count <= 4)
        own = words_ref[2] == block % 2
        pl.when(own)(functools.partial(place, mine_ref, lane, part))
        pl.when(jnp.logical_not(own))(functools.partial(place, theirs_ref, lane, part))
        for which in range(groups):
            group = block * groups + which

            @pl.when(words_ref[3] == group % blk_count)
            def _(part=part[:, which * HALF : (which + 1) * HALF], lane=group // blk_count * HALF):
                mine_ref[:, lane : lane + HALF] = jnp.where(even, part[:half], part[half:])
                theirs_ref[:, lane : lane + HALF] = jnp.where(even, part[half:], part[:half])


def other_parts(words, chosen, first, tp_count, blk_count, after):
    rows, width = first[0].shape
    lanes = tp_count * (width // HALF) // blk_count * HALF + tp_count // 2 * 2 * width
    return call(
        functools.partial(other_parts_kernel, tp_count, blk_count),
        [((rows // 2, lanes), jnp.float32)] * 2,
        [SMEM, VMEM, ANYWHERE] + [VMEM] * len(first),
        2 * (tp_count - 1 - len(first)),
        "other_parts",
        vmem=16 if tp_count <= 4 else 48,
    )(words, chosen, after, *first)


def group_at(rows, index, count):
    found = rows[:, :HALF]
    for place in range(1, count):
        found = jnp.where(index == place, rows[:, place * HALF : (place + 1) * HALF], found)
    return found


def halve_kernel(ex_count, bit, words_ref, left_ref, right_ref, keep_ref, send_ref):
    row_lanes = ex_count * HALF
    upper = words_ref[4] & bit != 0
    rows = left_ref[:, :row_lanes] + right_ref[:, :row_lanes]
    columns = left_ref[:, row_lanes:] + right_ref[:, row_lanes:]
    middle = columns.shape[1] // 2
    lanes = keep_ref.shape[1] - middle
    if bit > 2:
        keep_ref[:, :lanes] = rows
        send_ref[:, :lanes] = rows
    else:
        for step in range(1, ex_count):
            place = slice((step - 1) * HALF, step * HALF)
            keep_ref[:, place] = group_at(rows, words_ref[4] // 2 ^ step, ex_count)
            send_ref[:, place] = group_at(rows, words_ref[4] // 2 ^ 1 ^ step, ex_count)
    keep_ref[:, lanes:] = jnp.where(upper, columns[:, middle:], columns[:, :middle])
    send_ref[:, lanes:] = jnp.where(upper, columns[:, :middle], columns[:, middle:])


def halve(words, left, right, ex_count, bit):
    lanes = (ex_count if bit > 2 else ex_count - 1) * HALF
    shape = (left.shape[0], (left.shape[1] - ex_count * HALF) // 2 + lanes)
    return call(
        functools.partial(halve_kernel, ex_count, bit),
        [(shape, jnp.float32)] * 2,
        [SMEM, VMEM, VMEM],
        0.5,
        "halve",
    )(words, left, right)


def pieces_kernel(ex_count, scaling, words_ref, left_ref, right_ref, _, *piece_refs):
    total = ((left_ref[...] + right_ref[...]) * scaling).astype(jnp.bfloat16)
    for step, ref in enumerate(piece_refs):
        ref[:, :HALF] = group_at(total, (words_ref[5] ^ step ^ (words_ref[4] // 2)) - 1, ex_count - 1)
        ref[:, HALF:] = total[:, (ex_count - 1) * HALF :]


def pieces(words, left, right, ex_count, scaling, after):
    shape = (left.shape[0], left.shape[1] - (ex_count - 2) * HALF)
    return call(
        functools.partial(pieces_kernel, ex_count, scaling),
        [(shape, jnp.bfloat16)] * ex_count,
        [SMEM, VMEM, VMEM, ANYWHERE],
        0.5,
        "pieces",
    )(words, left, right, after)


def tdot(left, right):
    return lax.dot_general(left, right, (((0,), (0,)), ((), ())), preferred_element_type=jnp.float32)


def row_of(value, row):
    return jnp.broadcast_to(value[row : row + 1, :], value.shape)


def factor_stripe(rows_u, rows_z, offset):
    groups = len(rows_u)
    sub = lax.broadcasted_iota(jnp.int32, (8, BLOCK), 0)
    rows_u, rows_z = list(rows_u), list(rows_z)
    pivots = [jnp.ones((8, BLOCK), jnp.float32) for _ in range(groups)]
    for base in range(0, 8 * groups, SUB):
        columns = {
            c: {
                v: jnp.broadcast_to(rows_u[v][:, offset + c : offset + c + 1], (8, BLOCK))
                for v in range(c // 8, groups)
            }
            for c in range(base, base + SUB)
        }
        pivot = row_of(columns[base][base // 8], 0)
        for j in range(base, base + SUB):
            g, s = divmod(j, 8)
            column = columns[j]
            inverse = 1.0 / pivot
            pivots[g] = jnp.where(sub == s, pivot, pivots[g])
            if j + 1 < base + SUB:
                n, r = divmod(j + 1, 8)
                weight = row_of(column[n], r)
                following = columns[j + 1]
                pivot = row_of(following[n], r) - (weight * weight) * inverse
                for v in range(n, groups):
                    following[v] = following[v] - (column[v] * weight) * inverse
            factors = {v: column[v] * inverse for v in range(g, groups)}
            for c in range(j + 2, base + SUB):
                weight = row_of(column[c // 8], c % 8)
                for v in range(c // 8, groups):
                    columns[c][v] = columns[c][v] - factors[v] * weight
            factors[g] = jnp.where(sub > s, factors[g], 0.0)
            row_u, row_z = row_of(rows_u[g], s), row_of(rows_z[g], s)
            for v in range(g + (s == 7), groups):
                rows_u[v] = rows_u[v] - factors[v] * row_u
                rows_z[v] = rows_z[v] - factors[v] * row_z
    scales = [lax.rsqrt(pivot) for pivot in pivots]
    return (
        [row * scale for row, scale in zip(rows_u, scales)],
        [row * scale for row, scale in zip(rows_z, scales)],
    )


def thirds(value):
    high = value.astype(jnp.bfloat16)
    rest = value - high.astype(jnp.float32)
    middle = rest.astype(jnp.bfloat16)
    return high, middle, (rest - middle.astype(jnp.float32)).astype(jnp.bfloat16)


def exact_dot(left, right, axes=(1, 0)):
    left_parts, right_parts = thirds(left), thirds(right)
    terms = ((0, 0), (0, 1), (1, 0), (0, 2), (2, 0), (1, 1))
    count = max(1, min(len(terms), DEPTH // left.shape[axes[0]]))
    total = None
    for start in range(0, len(terms), count):
        some = terms[start : start + count]
        term = lax.dot_general(
            join([left_parts[i] for i, _ in some], axes[0]),
            join([right_parts[j] for _, j in some], axes[1]),
            (((axes[0],), (axes[1],)), ((), ())),
            preferred_element_type=jnp.float32,
        )
        total = term if total is None else total + term
    return total


def identity_mask(shape):
    return lax.broadcasted_iota(jnp.int32, shape, 0) == lax.broadcasted_iota(jnp.int32, shape, 1)


def factor_block(block):
    unit = identity_mask(block.shape).astype(jnp.float32)
    rows_u = [block[8 * v : 8 * v + 8] for v in range(BLOCK // 8)]
    rows_z = [unit[8 * v : 8 * v + 8] for v in range(BLOCK // 8)]
    groups = STRIPE // 8
    done = []
    for end in range(STRIPE, BLOCK + 1, STRIPE):
        upper, inverse = factor_stripe(rows_u[:groups], rows_z[:groups], end - STRIPE)
        done += inverse
        if end < BLOCK:
            upper, inverse = jnp.concatenate(upper, axis=0), jnp.concatenate(inverse, axis=0)
            update = exact_dot(upper, jnp.concatenate([upper, inverse], axis=1), (0, 0))[end:]
            rows_u = [row - update[8 * v : 8 * v + 8, :BLOCK] for v, row in enumerate(rows_u[groups:])]
            rows_z = [row - update[8 * v : 8 * v + 8, BLOCK:] for v, row in enumerate(rows_z[groups:])]
    return jnp.concatenate(done, axis=0)


def in_pair_order(even, refs, lanes=slice(None)):
    values = [ref[:, lanes] for ref in refs]
    count = len(values) // 2
    mine, other = join(values[:count], 0), join(values[count:], 0)
    return join([jnp.where(even, mine, other), jnp.where(even, other, mine)], 0)


def eliminate(gram, turned, upper_refs, done_refs, rest_refs):
    square = (BLOCK, BLOCK)
    keep = lax.broadcasted_iota(jnp.int32, square, 0) <= lax.broadcasted_iota(jnp.int32, square, 1)
    block = gram[:BLOCK, :BLOCK]
    for index, (upper_ref, done_ref) in enumerate(zip(upper_refs, done_refs)):
        inverse = factor_block(block)
        if index + 1 < len(upper_refs):
            beside = exact_dot(inverse, gram[:BLOCK, BLOCK : 2 * BLOCK])
            ahead = gram[BLOCK : 2 * BLOCK, BLOCK : 2 * BLOCK] - exact_dot(beside, beside, (0, 0))
        upper_ref[:, :BLOCK] = jnp.where(keep, exact_dot(inverse, block), 0.0)
        done = exact_dot(turned[:, :BLOCK], inverse, (1, 1))
        done_ref[...] = done
        if gram.shape[0] > BLOCK:
            rest = exact_dot(inverse, gram[:BLOCK, BLOCK:])
            upper_ref[:, BLOCK:] = rest
            gram = gram[BLOCK:, BLOCK:] - exact_dot(rest, rest, (0, 0))
            turned = turned[:, BLOCK:] - exact_dot(done, rest)
        if index + 1 < len(upper_refs):
            block = ahead
    if rest_refs:
        rest_refs[0][...] = gram
        rest_refs[1][...] = turned


def first_blocks_kernel(blocks, count, words_ref, ridge_ref, *refs):
    phi_refs, out_refs = refs[:count], refs[count:]
    phi = in_pair_order(words_ref[2] == 0, phi_refs)
    examples, width = phi.shape
    gram = tdot(phi, phi) * (1.0 / examples) + jnp.where(identity_mask((width, width)), ridge_ref[0], 0.0)
    eliminate(
        gram, phi.astype(jnp.float32), out_refs[:blocks], out_refs[blocks : 2 * blocks], out_refs[2 * blocks :]
    )


def next_blocks_kernel(blocks, gram_ref, turned_ref, *refs):
    eliminate(gram_ref[...], turned_ref[...], refs[:blocks], refs[blocks : 2 * blocks], refs[2 * blocks :])


def block_shapes(width, examples, blocks):
    rest = width - blocks * BLOCK
    shapes = [(BLOCK, width - index * BLOCK) for index in range(blocks)] + [(examples, BLOCK)] * blocks
    if rest:
        shapes += [(rest, rest), (examples, rest)]
    return [(shape, jnp.float32) for shape in shapes]


def taken_apart(results, blocks):
    return list(results[:blocks]), list(results[blocks : 2 * blocks]), results[2 * blocks :]


def first_blocks(words, ridge_value, phi, blocks):
    examples, width = sum(part.shape[0] for part in phi), phi[0].shape[1]
    results = call(
        functools.partial(first_blocks_kernel, blocks, len(phi)),
        block_shapes(width, examples, blocks),
        [SMEM, SMEM] + [VMEM] * len(phi),
        3.5,
        "gram_first_blocks",
    )(words, ridge_value, *phi)
    return taken_apart(results, blocks)


def next_blocks(rest, blocks):
    gram, turned = rest
    results = call(
        functools.partial(next_blocks_kernel, blocks),
        block_shapes(gram.shape[0], turned.shape[0], blocks),
        [VMEM, VMEM],
        4 * blocks,
        "eliminate_blocks",
    )(gram, turned)
    return taken_apart(results, blocks)


def finish_kernel(blocks, count, words_ref, ridge_ref, *refs):
    uppers, dones = refs[:blocks], refs[blocks : 2 * blocks]
    phi_refs, piece_refs = refs[2 * blocks : 2 * blocks + count], refs[2 * blocks + count : -3]
    panel_ref, trailing_ref, solved_ref = refs[-3:]
    height, panel = panel_ref.shape
    width = trailing_ref.shape[1]
    even = words_ref[2] == 0
    row_group, column_block = words_ref[6], words_ref[4]
    phi = in_pair_order(even, phi_refs)
    examples = phi.shape[0]
    mine, others = piece_refs[: count // 2], piece_refs[count // 2 :]
    columns, pair_columns = (
        join([ref[:, start : start + width] for start in (height, height + width) for ref in some], 0)
        for some in (mine, others)
    )
    rows = in_pair_order(even, piece_refs, slice(0, height))
    groups = width // height
    holder = words_ref[3] // groups
    held = jnp.where(holder == words_ref[2], columns, pair_columns)
    for place in range(groups):
        inside = (words_ref[5] == column_block // 2) & (words_ref[3] % groups == place)
        rows = jnp.where(inside, held[:, place * height : (place + 1) * height], rows)
    for start in range(0, panel, height):
        rows = jnp.where(row_group * height == start, phi[:, start : start + height], rows)
    columns = jnp.where(column_block == 0, phi, columns)
    turned = jnp.concatenate([rows, columns], axis=1).T
    parts = join(list(thirds(join([ref[...] for ref in dones], 1))), 0)
    scale = 1.0 / examples
    solved = jnp.dot(join([turned] * 3, 1), parts, preferred_element_type=jnp.float32) * scale
    panel_ref[...] = solved[:height]
    solved_ref[...] = solved[height:]

    def lower(row, lane):
        if row < lane:
            return jnp.zeros((BLOCK, BLOCK), jnp.float32)
        return uppers[lane // BLOCK][:, row - lane : row - lane + BLOCK].T

    def put(ref, first):
        for row in range(0, ref.shape[0], BLOCK):
            for lane in range(0, panel, BLOCK):
                ref[row : row + BLOCK, lane : lane + BLOCK] = lower(first + row, lane)

    pl.when(column_block == 0)(functools.partial(put, solved_ref, 0))
    for group in range(panel // height):
        pl.when(row_group == group)(functools.partial(put, panel_ref, group * height))
    shape = (height, width)
    diagonal = row_group * height + lax.broadcasted_iota(
        jnp.int32, shape, 0
    ) == column_block * width + lax.broadcasted_iota(jnp.int32, shape, 1)
    gram = jnp.dot(turned[:height], columns, preferred_element_type=jnp.float32) * scale
    trailing_ref[...] = (
        gram + jnp.where(diagonal, ridge_ref[0], 0.0) - exact_dot(panel_ref[...], solved_ref[...], (1, 1))
    )


def finish(words, ridge_value, uppers, dones, phi, gathered, height, width):
    panel = uppers[0].shape[1]
    operands = [*uppers, *dones, *phi, *gathered]
    return call(
        functools.partial(finish_kernel, len(uppers), len(phi)),
        [((height, panel), jnp.float32), ((height, width), jnp.float32)],
        [SMEM, SMEM] + [VMEM] * len(operands),
        3,
        "finish",
        [pltpu.VMEM((width, panel), jnp.float32)],
        vmem=24,
    )(words, ridge_value, *operands)


def swapped(value, axis, bit):
    return lax.ppermute(value, axis, [(s, s ^ bit) for s in range(lax.axis_size(axis))])


def ex_parts(own):
    return [own[0]] + [swapped(own[step], "ex", step) for step in range(1, lax.axis_size("ex"))]


def with_pair(parts):
    return list(parts) + [swapped(part, "tp", 1) for part in parts]


def shards(gradients, selection, seed_value, ridge_value):
    ex_count = lax.axis_size("ex")
    tp_count = lax.axis_size("tp")
    blk_count = lax.axis_size("blk")
    ex_index, tp_index, blk_index = (lax.axis_index(axis) for axis in ("ex", "tp", "blk"))
    coord_dev = gradients.shape[1]
    column_width = HALF * ex_count * blk_count // tp_count
    scaling = 1.0 / math.sqrt(coord_dev * tp_count)
    words = jnp.stack(
        [
            seed_value[0],
            tp_index * coord_dev,
            tp_index % 2,
            blk_index,
            tp_index,
            ex_index,
            ex_index * blk_count + blk_index,
        ]
    ).astype(jnp.int32)

    mine, theirs, chosen = panel_part(words, selection, gradients)
    total = mine + swapped(theirs, "tp", 1)
    halves = total
    bit = 2
    while bit < tp_count:
        total = total + swapped(total, "tp", bit)
        bit *= 2
    phi = ex_parts([(total * scaling).astype(jnp.bfloat16)] * ex_count)

    first = blocks_part(words, chosen, range(1, 1 + tp_count // 2), column_width, halves)
    left, right = other_parts(words, chosen, first, tp_count, blk_count, total)
    phi[1:], right = lax.optimization_barrier((phi[1:], right))
    right = swapped(right, "tp", 1)
    bit = tp_count // 2
    while bit > 1:
        left, right = halve(words, left, right, ex_count, bit)
        right = swapped(right, "tp", bit)
        bit //= 2

    phi = with_pair(phi)
    half = PANEL // BLOCK // 2
    uppers, dones, rest = first_blocks(words, ridge_value, phi, half)
    gathered = pieces(words, left, right, ex_count, scaling, dones[-1])
    gathered = with_pair(ex_parts(gathered))
    while rest:
        more_uppers, more_dones, rest = next_blocks(rest, 1)
        uppers, dones = uppers + more_uppers, dones + more_dones
    return tuple(finish(words, ridge_value, uppers, dones, phi, gathered, HALF, column_width))


def solution(mesh):
    in_specs = (P("ex", "tp"), P("ex"), P(), P())
    out_specs = (P(("ex", "blk"), None), P(("ex", "blk"), "tp"))
    return jax.shard_map(shards, mesh=mesh, in_specs=in_specs, out_specs=out_specs, check_vma=False)
```

```python
import functools
import math

import jax
import jax.numpy as jnp
from jax import lax
from jax.experimental import pallas as pl
from jax.experimental.pallas import tpu as pltpu
from jax.sharding import PartitionSpec as P

PANEL = 512
HALF = 256
STRIPE = 64
SUB = 8
LEAD = 3
BLOCK = 128
DEPTH = 256
SEGMENT = 128
VMEM = pl.BlockSpec(memory_space=pltpu.VMEM)
ANYWHERE = pl.BlockSpec(memory_space=pl.ANY)


def call(kernel, out_shape, in_specs, microseconds, name, scratch=(), vmem=16):
    shapes = [jax.ShapeDtypeStruct(shape, dtype) for shape, dtype in out_shape]
    return pl.pallas_call(
        kernel,
        out_shape=shapes,
        in_specs=in_specs,
        out_specs=[VMEM] * len(shapes),
        scratch_shapes=list(scratch),
        compiler_params=pltpu.CompilerParams(vmem_limit_bytes=vmem * 1024 * 1024),
        cost_estimate=pl.CostEstimate(
            flops=int(microseconds * 1_100_000_000), bytes_accessed=1_000_000, transcendentals=0
        ),
        name=name,
    )


def join(parts, axis):
    return parts[0] if len(parts) == 1 else jnp.concatenate(parts, axis)


def shifted(value, amount):
    return lax.shift_right_logical(value, jnp.full_like(value, amount))


def sign_tile(seed_word, coordinate, feature, shape):
    rows = (lax.broadcasted_iota(jnp.int32, (shape[0], 1), 0) + coordinate) * jnp.int32(-1640531535)
    columns = (lax.broadcasted_iota(jnp.int32, (1, shape[1]), 1) + feature) * jnp.int32(668265263) + seed_word
    hashed = rows + columns
    hashed = (hashed ^ shifted(hashed, 16)) * jnp.int32(-2048144789)
    hashed = (hashed ^ shifted(hashed, 13)) * jnp.int32(-1028477387)
    decided = (hashed ^ shifted(hashed, 16)).astype(jnp.int16) & jnp.int16(128)
    return jnp.where(decided == 0, jnp.bfloat16(1.0), jnp.bfloat16(-1.0))


def segment_signs(seed_ref, coordinates, feature, width, index):
    first = lax.axis_index("tp") * coordinates + index * SEGMENT
    return sign_tile(seed_ref[...], first, feature, (SEGMENT, width))


def project_step(seed_ref, chosen_ref, feature, width, index, total):
    start = pl.multiple_of(index * SEGMENT, SEGMENT)
    signs = segment_signs(seed_ref, chosen_ref.shape[1], feature, width, index)
    return total + jnp.dot(chosen_ref[:, pl.ds(start, SEGMENT)], signs, preferred_element_type=jnp.float32)


def project_tile(seed_ref, chosen_ref, feature, width, unroll):
    rows, coordinates = chosen_ref.shape
    step = functools.partial(project_step, seed_ref, chosen_ref, feature, width)
    zero = jnp.zeros((rows, width), jnp.float32)
    return lax.fori_loop(0, coordinates // SEGMENT, step, zero, unroll=unroll)


def even_of_pair():
    return lax.axis_index("tp") % 2 == 0


def panel_signs_kernel(seed_ref, signs_ref):
    coordinates, width = signs_ref.shape
    for step in range(coordinates // SEGMENT):
        signs_ref[step * SEGMENT : (step + 1) * SEGMENT, :] = segment_signs(
            seed_ref, coordinates, 0, width, step
        )


def panel_signs(seed, coordinates):
    return call(
        panel_signs_kernel, [((coordinates, PANEL), jnp.bfloat16)], [VMEM], 2, "panel_signs"
    )(seed)[0]


def panel_part_kernel(selection_ref, pool_ref, signs_ref, mine_ref, theirs_ref, chosen_ref):
    half = mine_ref.shape[0]
    shape = (pool_ref.shape[0], chosen_ref.shape[0])
    picked = jnp.where(lax.broadcasted_iota(jnp.int32, shape, 0) == selection_ref[...], 1.0, 0.0)
    chosen = tdot(picked.astype(jnp.bfloat16), pool_ref[...]).astype(jnp.bfloat16)
    chosen_ref[...] = chosen
    total = jnp.dot(chosen, signs_ref[...], preferred_element_type=jnp.float32)
    even = even_of_pair()
    mine_ref[...] = jnp.where(even, total[:half], total[half:])
    theirs_ref[...] = jnp.where(even, total[half:], total[:half])


def panel_part(seed, selection, pool):
    rows, coordinates = selection.shape[0], pool.shape[1]
    return call(
        panel_part_kernel,
        [((rows // 2, PANEL), jnp.float32)] * 2 + [((rows, coordinates), jnp.bfloat16)],
        [VMEM, VMEM, VMEM],
        1,
        "panel_part",
    )(selection[None, :], pool, panel_signs(seed, coordinates))


def blocks_part_kernel(blocks, seed_ref, chosen_ref, _, *part_refs):
    width = part_refs[0].shape[1]
    for block, part_ref in zip(blocks, part_refs):
        part_ref[...] = project_tile(seed_ref, chosen_ref, block * width, width, len(blocks) <= 2)


def blocks_part(seed, chosen, blocks, width, after):
    return call(
        functools.partial(blocks_part_kernel, blocks),
        [((chosen.shape[0], width), jnp.float32)] * len(blocks),
        [VMEM, VMEM, ANYWHERE],
        2 * len(blocks),
        "blocks_part",
        vmem=32 if len(blocks) > 2 else 16,
    )(seed, chosen, after)


def other_parts_kernel(tp_count, blk_count, seed_ref, chosen_ref, _, *refs):
    *first_refs, mine_ref, theirs_ref = refs
    rows = chosen_ref.shape[0]
    half = rows // 2
    width = first_refs[0].shape[1]
    groups = width // HALF
    row_lanes = tp_count * groups // blk_count * HALF
    even = even_of_pair()
    for ref in (mine_ref, theirs_ref):
        ref[:, : row_lanes + 2 * width] = jnp.zeros((half, row_lanes + 2 * width), jnp.float32)

    def place(ref, lane, part):
        ref[:, lane : lane + width] = part[:half]
        ref[:, lane + width : lane + 2 * width] = part[half:]

    for block in range(1, tp_count):
        lane = row_lanes + block // 2 * 2 * width
        if block <= len(first_refs):
            part = first_refs[block - 1][...]
        else:
            part = project_tile(seed_ref, chosen_ref, block * width, width, tp_count <= 4)
        own = lax.axis_index("tp") % 2 == block % 2
        pl.when(own)(functools.partial(place, mine_ref, lane, part))
        pl.when(jnp.logical_not(own))(functools.partial(place, theirs_ref, lane, part))
        for which in range(groups):
            group = block * groups + which

            @pl.when(lax.axis_index("blk") == group % blk_count)
            def _(part=part[:, which * HALF : (which + 1) * HALF], lane=group // blk_count * HALF):
                mine_ref[:, lane : lane + HALF] = jnp.where(even, part[:half], part[half:])
                theirs_ref[:, lane : lane + HALF] = jnp.where(even, part[half:], part[:half])


def other_parts(seed, chosen, first, tp_count, blk_count, after):
    rows, width = first[0].shape
    lanes = tp_count * (width // HALF) // blk_count * HALF + tp_count // 2 * 2 * width
    return call(
        functools.partial(other_parts_kernel, tp_count, blk_count),
        [((rows // 2, lanes), jnp.float32)] * 2,
        [VMEM, VMEM, ANYWHERE] + [VMEM] * len(first),
        2 * (tp_count - 1 - len(first)),
        "other_parts",
        vmem=16 if tp_count <= 4 else 48,
    )(seed, chosen, after, *first)


def group_at(rows, index, count):
    found = rows[:, :HALF]
    for place in range(1, count):
        found = jnp.where(index == place, rows[:, place * HALF : (place + 1) * HALF], found)
    return found


def halve_kernel(ex_count, bit, left_ref, right_ref, keep_ref, send_ref):
    row_lanes = ex_count * HALF
    upper = lax.axis_index("tp") & bit != 0
    total = left_ref[...] + right_ref[...]
    middle = (total.shape[1] + row_lanes) // 2
    keep_ref[:, :row_lanes] = total[:, :row_lanes]
    send_ref[:, :row_lanes] = total[:, :row_lanes]
    keep_ref[:, row_lanes:] = jnp.where(upper, total[:, middle:], total[:, row_lanes:middle])
    send_ref[:, row_lanes:] = jnp.where(upper, total[:, row_lanes:middle], total[:, middle:])


def halve(left, right, ex_count, bit):
    shape = (left.shape[0], (left.shape[1] + ex_count * HALF) // 2)
    return call(
        functools.partial(halve_kernel, ex_count, bit),
        [(shape, jnp.float32)] * 2,
        [VMEM, VMEM],
        0.5,
        "halve",
    )(left, right)


def last_half(ex_count, holder, left_ref, right_ref):
    def picked(index, places):
        found = None
        for place, lanes in enumerate(places):
            value = (left_ref[:, lanes], right_ref[:, lanes])
            if found is None:
                found = value
            else:
                found = tuple(jnp.where(index == place, new, old) for new, old in zip(value, found))
        return found[0] + found[1]

    groups = [slice(place * HALF, (place + 1) * HALF) for place in range(ex_count)]
    row_lanes = ex_count * HALF
    middle = (left_ref.shape[1] + row_lanes) // 2
    blocks = [slice(row_lanes, middle), slice(middle, left_ref.shape[1])]
    rows = [picked(holder ^ step, groups) for step in range(1, ex_count)]
    return rows, picked(holder & 1, blocks)


def send_kernel(ex_count, left_ref, right_ref, send_ref):
    rows, columns = last_half(ex_count, lax.axis_index("tp") // 2 ^ 1, left_ref, right_ref)
    lanes = (ex_count - 1) * HALF
    send_ref[:, :lanes] = join(rows, 1)
    send_ref[:, lanes:] = columns


def last_sent(left, right, ex_count):
    row_lanes = ex_count * HALF
    shape = (left.shape[0], (left.shape[1] - row_lanes) // 2 + row_lanes - HALF)
    return call(
        functools.partial(send_kernel, ex_count),
        [(shape, jnp.float32)],
        [VMEM, VMEM],
        0.5,
        "last_sent",
    )(left, right)[0]


def pieces_kernel(ex_count, scaling, left_ref, right_ref, came_ref, _, *piece_refs):
    holder = lax.axis_index("tp") // 2
    rows, columns = last_half(ex_count, holder, left_ref, right_ref)
    rows = [
        ((row + came_ref[:, place * HALF : (place + 1) * HALF]) * scaling).astype(jnp.bfloat16)
        for place, row in enumerate(rows)
    ]
    columns = ((columns + came_ref[:, (ex_count - 1) * HALF :]) * scaling).astype(jnp.bfloat16)
    for step, ref in enumerate(piece_refs):
        distance = lax.axis_index("ex") ^ step ^ holder
        wanted = rows[0]
        for place in range(1, ex_count - 1):
            wanted = jnp.where(distance - 1 == place, rows[place], wanted)
        ref[:, :HALF] = wanted
        ref[:, HALF:] = columns


def pieces(left, right, came, ex_count, scaling, after):
    shape = (left.shape[0], came.shape[1] - (ex_count - 2) * HALF)
    return call(
        functools.partial(pieces_kernel, ex_count, scaling),
        [(shape, jnp.bfloat16)] * ex_count,
        [VMEM, VMEM, VMEM, ANYWHERE],
        0.5,
        "pieces",
    )(left, right, came, after)


def tdot(left, right):
    return lax.dot_general(left, right, (((0,), (0,)), ((), ())), preferred_element_type=jnp.float32)


def row_of(value, row):
    return jnp.broadcast_to(value[row : row + 1, :], value.shape)


def factor_stripe(rows_u, rows_z, offset):
    groups = len(rows_u)
    count = 8 * groups
    sub = lax.broadcasted_iota(jnp.int32, (8, BLOCK), 0)
    rows_u, rows_z = list(rows_u), list(rows_z)
    pivots = [jnp.ones((8, BLOCK), jnp.float32) for _ in range(groups)]

    def taken(base):
        return {
            c: {
                v: jnp.broadcast_to(rows_u[v][:, offset + c : offset + c + 1], (8, BLOCK))
                for v in range(c // 8, groups)
            }
            for c in range(base, base + SUB)
        }

    columns = taken(0)
    pivot = row_of(columns[0][0], 0)
    for j in range(count):
        g, s = divmod(j, 8)
        if j % SUB == SUB - LEAD and j + LEAD < count:
            columns.update(taken(j + LEAD))
        column = columns.pop(j)
        inverse = 1.0 / pivot
        pivots[g] = jnp.where(sub == s, pivot, pivots[g])
        if j + 1 < count:
            n, r = divmod(j + 1, 8)
            weight = row_of(column[n], r)
            following = columns[j + 1]
            pivot = row_of(following[n], r) - (weight * weight) * inverse
            for v in range(n, groups):
                following[v] = following[v] - (column[v] * weight) * inverse
        factors = {v: column[v] * inverse for v in range(g, groups)}
        for c, other in columns.items():
            if c > j + 1:
                weight = row_of(column[c // 8], c % 8)
                for v in range(c // 8, groups):
                    other[v] = other[v] - factors[v] * weight
        factors[g] = jnp.where(sub > s, factors[g], 0.0)
        row_u, row_z = row_of(rows_u[g], s), row_of(rows_z[g], s)
        for v in range(g + (s == 7), groups):
            rows_u[v] = rows_u[v] - factors[v] * row_u
            rows_z[v] = rows_z[v] - factors[v] * row_z
    scales = [lax.rsqrt(pivot) for pivot in pivots]
    return (
        [row * scale for row, scale in zip(rows_u, scales)],
        [row * scale for row, scale in zip(rows_z, scales)],
    )


def thirds(value):
    high = value.astype(jnp.bfloat16)
    rest = value - high.astype(jnp.float32)
    middle = rest.astype(jnp.bfloat16)
    return high, middle, (rest - middle.astype(jnp.float32)).astype(jnp.bfloat16)


def exact_dot(left, right, axes=(1, 0)):
    left_parts, right_parts = thirds(left), thirds(right)
    terms = ((0, 0), (0, 1), (1, 0), (0, 2), (2, 0), (1, 1))
    count = max(1, min(len(terms), DEPTH // left.shape[axes[0]]))
    total = None
    for start in range(0, len(terms), count):
        some = terms[start : start + count]
        term = lax.dot_general(
            join([left_parts[i] for i, _ in some], axes[0]),
            join([right_parts[j] for _, j in some], axes[1]),
            (((axes[0],), (axes[1],)), ((), ())),
            preferred_element_type=jnp.float32,
        )
        total = term if total is None else total + term
    return total


def identity_mask(shape):
    return lax.broadcasted_iota(jnp.int32, shape, 0) == lax.broadcasted_iota(jnp.int32, shape, 1)


def factor_block(block):
    unit = identity_mask(block.shape).astype(jnp.float32)
    rows_u = [block[8 * v : 8 * v + 8] for v in range(BLOCK // 8)]
    rows_z = [unit[8 * v : 8 * v + 8] for v in range(BLOCK // 8)]
    groups = STRIPE // 8
    done = []
    for end in range(STRIPE, BLOCK + 1, STRIPE):
        upper, inverse = factor_stripe(rows_u[:groups], rows_z[:groups], end - STRIPE)
        done += inverse
        if end < BLOCK:
            upper, inverse = jnp.concatenate(upper, axis=0), jnp.concatenate(inverse, axis=0)
            update = exact_dot(upper, jnp.concatenate([upper, inverse], axis=1), (0, 0))[end:]
            rows_u = [row - update[8 * v : 8 * v + 8, :BLOCK] for v, row in enumerate(rows_u[groups:])]
            rows_z = [row - update[8 * v : 8 * v + 8, BLOCK:] for v, row in enumerate(rows_z[groups:])]
    return jnp.concatenate(done, axis=0)


def in_pair_order(even, refs, lanes=slice(None)):
    values = [ref[:, lanes] for ref in refs]
    count = len(values) // 2
    mine, other = join(values[:count], 0), join(values[count:], 0)
    return join([jnp.where(even, mine, other), jnp.where(even, other, mine)], 0)


def eliminate(gram, turned, upper_refs, done_refs, rest_refs):
    square = (BLOCK, BLOCK)
    keep = lax.broadcasted_iota(jnp.int32, square, 0) <= lax.broadcasted_iota(jnp.int32, square, 1)
    block = gram[:BLOCK, :BLOCK]
    for index, (upper_ref, done_ref) in enumerate(zip(upper_refs, done_refs)):
        inverse = factor_block(block)
        if index + 1 < len(upper_refs):
            beside = exact_dot(inverse, gram[:BLOCK, BLOCK : 2 * BLOCK])
            ahead = gram[BLOCK : 2 * BLOCK, BLOCK : 2 * BLOCK] - exact_dot(beside, beside, (0, 0))
        upper_ref[:, :BLOCK] = jnp.where(keep, exact_dot(inverse, block), 0.0)
        done = exact_dot(turned[:, :BLOCK], inverse, (1, 1))
        done_ref[...] = done
        if gram.shape[0] > BLOCK:
            rest = exact_dot(inverse, gram[:BLOCK, BLOCK:])
            upper_ref[:, BLOCK:] = rest
            gram = gram[BLOCK:, BLOCK:] - exact_dot(rest, rest, (0, 0))
            turned = turned[:, BLOCK:] - exact_dot(done, rest)
        if index + 1 < len(upper_refs):
            block = ahead
    if rest_refs:
        rest_refs[0][...] = gram
        rest_refs[1][...] = turned


def first_blocks_kernel(blocks, count, ridge_ref, *refs):
    phi_refs, out_refs = refs[:count], refs[count:]
    phi = in_pair_order(even_of_pair(), phi_refs)
    examples, width = phi.shape
    gram = tdot(phi, phi) * (1.0 / examples) + jnp.where(identity_mask((width, width)), ridge_ref[...], 0.0)
    eliminate(
        gram, phi.astype(jnp.float32), out_refs[:blocks], out_refs[blocks : 2 * blocks], out_refs[2 * blocks :]
    )


def next_blocks_kernel(blocks, gram_ref, turned_ref, *refs):
    eliminate(gram_ref[...], turned_ref[...], refs[:blocks], refs[blocks : 2 * blocks], refs[2 * blocks :])


def block_shapes(width, examples, blocks):
    rest = width - blocks * BLOCK
    shapes = [(BLOCK, width - index * BLOCK) for index in range(blocks)] + [(examples, BLOCK)] * blocks
    if rest:
        shapes += [(rest, rest), (examples, rest)]
    return [(shape, jnp.float32) for shape in shapes]


def taken_apart(results, blocks):
    return list(results[:blocks]), list(results[blocks : 2 * blocks]), results[2 * blocks :]


def first_blocks(ridge, phi, blocks):
    examples, width = sum(part.shape[0] for part in phi), phi[0].shape[1]
    results = call(
        functools.partial(first_blocks_kernel, blocks, len(phi)),
        block_shapes(width, examples, blocks),
        [VMEM] * (1 + len(phi)),
        3.5,
        "gram_first_blocks",
    )(ridge, *phi)
    return taken_apart(results, blocks)


def next_blocks(rest, blocks):
    gram, turned = rest
    results = call(
        functools.partial(next_blocks_kernel, blocks),
        block_shapes(gram.shape[0], turned.shape[0], blocks),
        [VMEM, VMEM],
        4 * blocks,
        "eliminate_blocks",
    )(gram, turned)
    return taken_apart(results, blocks)


def finish_kernel(blocks, count, blk_count, ridge_ref, *refs):
    uppers, dones = refs[:blocks], refs[blocks : 2 * blocks]
    phi_refs, piece_refs = refs[2 * blocks : 2 * blocks + count], refs[2 * blocks + count : -3]
    panel_ref, trailing_ref, solved_ref = refs[-3:]
    height, panel = panel_ref.shape
    width = trailing_ref.shape[1]
    even = even_of_pair()
    ex_index, column_block, blk_index = (lax.axis_index(axis) for axis in ("ex", "tp", "blk"))
    row_group = ex_index * blk_count + blk_index
    phi = in_pair_order(even, phi_refs)
    examples = phi.shape[0]
    mine, others = piece_refs[: count // 2], piece_refs[count // 2 :]
    columns, pair_columns = (
        join([ref[:, start : start + width] for start in (height, height + width) for ref in some], 0)
        for some in (mine, others)
    )
    rows = in_pair_order(even, piece_refs, slice(0, height))
    groups = width // height
    holder = blk_index // groups
    held = jnp.where(holder == column_block % 2, columns, pair_columns)
    for place in range(groups):
        inside = (ex_index == column_block // 2) & (blk_index % groups == place)
        rows = jnp.where(inside, held[:, place * height : (place + 1) * height], rows)
    for start in range(0, panel, height):
        rows = jnp.where(row_group * height == start, phi[:, start : start + height], rows)
    columns = jnp.where(column_block == 0, phi, columns)
    turned = jnp.concatenate([rows, columns], axis=1).T
    parts = join(list(thirds(join([ref[...] for ref in dones], 1))), 0)
    scale = 1.0 / examples
    solved = jnp.dot(join([turned] * 3, 1), parts, preferred_element_type=jnp.float32) * scale
    panel_ref[...] = solved[:height]
    solved_ref[...] = solved[height:]

    def lower(row, lane):
        if row < lane:
            return jnp.zeros((BLOCK, BLOCK), jnp.float32)
        return uppers[lane // BLOCK][:, row - lane : row - lane + BLOCK].T

    def put(ref, first):
        for row in range(0, ref.shape[0], BLOCK):
            for lane in range(0, panel, BLOCK):
                ref[row : row + BLOCK, lane : lane + BLOCK] = lower(first + row, lane)

    pl.when(column_block == 0)(functools.partial(put, solved_ref, 0))
    for group in range(panel // height):
        pl.when(row_group == group)(functools.partial(put, panel_ref, group * height))
    shape = (height, width)
    diagonal = row_group * height + lax.broadcasted_iota(
        jnp.int32, shape, 0
    ) == column_block * width + lax.broadcasted_iota(jnp.int32, shape, 1)
    gram = jnp.dot(turned[:height], columns, preferred_element_type=jnp.float32) * scale
    trailing_ref[...] = (
        gram + jnp.where(diagonal, ridge_ref[...], 0.0) - exact_dot(panel_ref[...], solved_ref[...], (1, 1))
    )


def finish(ridge, uppers, dones, phi, gathered, height, width, blk_count):
    panel = uppers[0].shape[1]
    operands = [*uppers, *dones, *phi, *gathered]
    return call(
        functools.partial(finish_kernel, len(uppers), len(phi), blk_count),
        [((height, panel), jnp.float32), ((height, width), jnp.float32)],
        [VMEM] * (1 + len(operands)),
        3,
        "finish",
        [pltpu.VMEM((width, panel), jnp.float32)],
        vmem=24,
    )(ridge, *operands)


def swapped(value, axis, bit):
    return lax.ppermute(value, axis, [(s, s ^ bit) for s in range(lax.axis_size(axis))])


def ex_parts(own):
    return [own[0]] + [swapped(own[step], "ex", step) for step in range(1, lax.axis_size("ex"))]


def with_pair(parts):
    return list(parts) + [swapped(part, "tp", 1) for part in parts]


def shards(gradients, selection, seed_value, ridge_value):
    ex_count = lax.axis_size("ex")
    tp_count = lax.axis_size("tp")
    blk_count = lax.axis_size("blk")
    coord_dev = gradients.shape[1]
    column_width = HALF * ex_count * blk_count // tp_count
    scaling = 1.0 / math.sqrt(coord_dev * tp_count)
    seed, ridge = seed_value.reshape(1, 1), ridge_value.reshape(1, 1)

    mine, theirs, chosen = panel_part(seed, selection, gradients)
    total = mine + swapped(theirs, "tp", 1)
    halves = total
    bit = 2
    while bit < tp_count:
        total = total + swapped(total, "tp", bit)
        bit *= 2
    phi = ex_parts([(total * scaling).astype(jnp.bfloat16)] * ex_count)

    first = blocks_part(seed, chosen, range(1, 1 + tp_count // 2), column_width, halves)
    left, right = other_parts(seed, chosen, first, tp_count, blk_count, total)
    phi[1:], right = lax.optimization_barrier((phi[1:], right))
    right = swapped(right, "tp", 1)
    bit = tp_count // 2
    while bit > 2:
        left, right = halve(left, right, ex_count, bit)
        right = swapped(right, "tp", bit)
        bit //= 2
    came = swapped(last_sent(left, right, ex_count), "tp", 2)

    phi = with_pair(phi)
    half = PANEL // BLOCK // 2
    uppers, dones, rest = first_blocks(ridge, phi, half)
    gathered = pieces(left, right, came, ex_count, scaling, dones[-1])
    gathered = with_pair(ex_parts(gathered))
    while rest:
        more_uppers, more_dones, rest = next_blocks(rest, 1)
        uppers, dones = uppers + more_uppers, dones + more_dones
    return tuple(finish(ridge, uppers, dones, phi, gathered, HALF, column_width, blk_count))


def solution(mesh):
    in_specs = (P("ex", "tp"), P("ex"), P(), P())
    out_specs = (P(("ex", "blk"), None), P(("ex", "blk"), "tp"))
    return jax.shard_map(shards, mesh=mesh, in_specs=in_specs, out_specs=out_specs, check_vma=False)
```

```python
import functools
import math

import jax
import jax.numpy as jnp
from jax import lax
from jax.experimental import pallas as pl
from jax.experimental.pallas import tpu as pltpu
from jax.sharding import PartitionSpec as P

PANEL = 512
HALF = 256
STRIPE = 64
SUB = 8
LEAD = 3
BLOCK = 128
DEPTH = 256
SEGMENT = 128
VMEM = pl.BlockSpec(memory_space=pltpu.VMEM)
ANYWHERE = pl.BlockSpec(memory_space=pl.ANY)


def call(kernel, out_shape, in_specs, microseconds, name, scratch=(), vmem=16):
    shapes = [jax.ShapeDtypeStruct(shape, dtype) for shape, dtype in out_shape]
    return pl.pallas_call(
        kernel,
        out_shape=shapes,
        in_specs=in_specs,
        out_specs=[VMEM] * len(shapes),
        scratch_shapes=list(scratch),
        compiler_params=pltpu.CompilerParams(vmem_limit_bytes=vmem * 1024 * 1024),
        cost_estimate=pl.CostEstimate(
            flops=int(microseconds * 1_100_000_000), bytes_accessed=1_000_000, transcendentals=0
        ),
        name=name,
    )


def join(parts, axis):
    return parts[0] if len(parts) == 1 else jnp.concatenate(parts, axis)


def shifted(value, amount):
    return lax.shift_right_logical(value, jnp.full_like(value, amount))


def sign_tile(seed_word, coordinate, feature, shape):
    rows = (lax.broadcasted_iota(jnp.int32, (shape[0], 1), 0) + coordinate) * jnp.int32(-1640531535)
    columns = (lax.broadcasted_iota(jnp.int32, (1, shape[1]), 1) + feature) * jnp.int32(668265263) + seed_word
    hashed = rows + columns
    hashed = (hashed ^ shifted(hashed, 16)) * jnp.int32(-2048144789)
    hashed = (hashed ^ shifted(hashed, 13)) * jnp.int32(-1028477387)
    decided = (hashed ^ shifted(hashed, 16)).astype(jnp.int16) & jnp.int16(128)
    return jnp.where(decided == 0, jnp.bfloat16(1.0), jnp.bfloat16(-1.0))


def segment_signs(seed_ref, coordinates, feature, width, index):
    first = lax.axis_index("tp") * coordinates + index * SEGMENT
    return sign_tile(seed_ref[...], first, feature, (SEGMENT, width))


def project_step(seed_ref, chosen_ref, feature, width, index, total):
    start = pl.multiple_of(index * SEGMENT, SEGMENT)
    signs = segment_signs(seed_ref, chosen_ref.shape[1], feature, width, index)
    return total + jnp.dot(chosen_ref[:, pl.ds(start, SEGMENT)], signs, preferred_element_type=jnp.float32)


def project_tile(seed_ref, chosen_ref, feature, width, unroll):
    rows, coordinates = chosen_ref.shape
    step = functools.partial(project_step, seed_ref, chosen_ref, feature, width)
    zero = jnp.zeros((rows, width), jnp.float32)
    return lax.fori_loop(0, coordinates // SEGMENT, step, zero, unroll=unroll)


def even_of_pair():
    return lax.axis_index("tp") % 2 == 0


def panel_signs_kernel(seed_ref, signs_ref):
    coordinates, width = signs_ref.shape
    for step in range(coordinates // SEGMENT):
        signs_ref[step * SEGMENT : (step + 1) * SEGMENT, :] = segment_signs(
            seed_ref, coordinates, 0, width, step
        )


def panel_signs(seed, coordinates):
    return call(
        panel_signs_kernel, [((coordinates, PANEL), jnp.bfloat16)], [VMEM], 2, "panel_signs"
    )(seed)[0]


def panel_part_kernel(selection_ref, pool_ref, signs_ref, mine_ref, theirs_ref, chosen_ref):
    half = mine_ref.shape[0]
    shape = (pool_ref.shape[0], chosen_ref.shape[0])
    picked = jnp.where(lax.broadcasted_iota(jnp.int32, shape, 0) == selection_ref[...], 1.0, 0.0)
    chosen = tdot(picked.astype(jnp.bfloat16), pool_ref[...]).astype(jnp.bfloat16)
    chosen_ref[...] = chosen
    total = jnp.dot(chosen, signs_ref[...], preferred_element_type=jnp.float32)
    even = even_of_pair()
    mine_ref[...] = jnp.where(even, total[:half], total[half:])
    theirs_ref[...] = jnp.where(even, total[half:], total[:half])


def panel_part(seed, selection, pool):
    rows, coordinates = selection.shape[0], pool.shape[1]
    return call(
        panel_part_kernel,
        [((rows // 2, PANEL), jnp.float32)] * 2 + [((rows, coordinates), jnp.bfloat16)],
        [VMEM, VMEM, VMEM],
        1,
        "panel_part",
    )(selection[None, :], pool, panel_signs(seed, coordinates))


def blocks_part_kernel(blocks, seed_ref, chosen_ref, _, *part_refs):
    width = part_refs[0].shape[1]
    for block, part_ref in zip(blocks, part_refs):
        part_ref[...] = project_tile(seed_ref, chosen_ref, block * width, width, len(blocks) <= 2)


def blocks_part(seed, chosen, blocks, width, after):
    return call(
        functools.partial(blocks_part_kernel, blocks),
        [((chosen.shape[0], width), jnp.float32)] * len(blocks),
        [VMEM, VMEM, ANYWHERE],
        2 * len(blocks),
        "blocks_part",
        vmem=32 if len(blocks) > 2 else 16,
    )(seed, chosen, after)


def other_parts_kernel(tp_count, blk_count, seed_ref, chosen_ref, _, *refs):
    *first_refs, mine_ref, theirs_ref = refs
    rows = chosen_ref.shape[0]
    half = rows // 2
    width = first_refs[0].shape[1]
    groups = width // HALF
    row_lanes = tp_count * groups // blk_count * HALF
    even = even_of_pair()
    for ref in (mine_ref, theirs_ref):
        ref[:, : row_lanes + 2 * width] = jnp.zeros((half, row_lanes + 2 * width), jnp.float32)

    def place(ref, lane, part):
        ref[:, lane : lane + width] = part[:half]
        ref[:, lane + width : lane + 2 * width] = part[half:]

    for block in range(1, tp_count):
        lane = row_lanes + block // 2 * 2 * width
        if block <= len(first_refs):
            part = first_refs[block - 1][...]
        else:
            part = project_tile(seed_ref, chosen_ref, block * width, width, tp_count <= 4)
        own = lax.axis_index("tp") % 2 == block % 2
        pl.when(own)(functools.partial(place, mine_ref, lane, part))
        pl.when(jnp.logical_not(own))(functools.partial(place, theirs_ref, lane, part))
        for which in range(groups):
            group = block * groups + which

            @pl.when(lax.axis_index("blk") == group % blk_count)
            def _(part=part[:, which * HALF : (which + 1) * HALF], lane=group // blk_count * HALF):
                mine_ref[:, lane : lane + HALF] = jnp.where(even, part[:half], part[half:])
                theirs_ref[:, lane : lane + HALF] = jnp.where(even, part[half:], part[:half])


def other_parts(seed, chosen, first, tp_count, blk_count, after):
    rows, width = first[0].shape
    lanes = tp_count * (width // HALF) // blk_count * HALF + tp_count // 2 * 2 * width
    return call(
        functools.partial(other_parts_kernel, tp_count, blk_count),
        [((rows // 2, lanes), jnp.float32)] * 2,
        [VMEM, VMEM, ANYWHERE] + [VMEM] * len(first),
        2 * (tp_count - 1 - len(first)),
        "other_parts",
        vmem=16 if tp_count <= 4 else 48,
    )(seed, chosen, after, *first)


def group_at(rows, index, count):
    found = rows[:, :HALF]
    for place in range(1, count):
        found = jnp.where(index == place, rows[:, place * HALF : (place + 1) * HALF], found)
    return found


def halve_kernel(ex_count, bit, left_ref, right_ref, keep_ref, send_ref):
    row_lanes = ex_count * HALF
    upper = lax.axis_index("tp") & bit != 0
    total = left_ref[...] + right_ref[...]
    middle = (total.shape[1] + row_lanes) // 2
    keep_ref[:, :row_lanes] = total[:, :row_lanes]
    send_ref[:, :row_lanes] = total[:, :row_lanes]
    keep_ref[:, row_lanes:] = jnp.where(upper, total[:, middle:], total[:, row_lanes:middle])
    send_ref[:, row_lanes:] = jnp.where(upper, total[:, row_lanes:middle], total[:, middle:])


def halve(left, right, ex_count, bit):
    shape = (left.shape[0], (left.shape[1] + ex_count * HALF) // 2)
    return call(
        functools.partial(halve_kernel, ex_count, bit),
        [(shape, jnp.float32)] * 2,
        [VMEM, VMEM],
        0.5,
        "halve",
    )(left, right)


def last_half(ex_count, holder, left_ref, right_ref):
    def picked(index, places):
        found = None
        for place, lanes in enumerate(places):
            value = (left_ref[:, lanes], right_ref[:, lanes])
            if found is None:
                found = value
            else:
                found = tuple(jnp.where(index == place, new, old) for new, old in zip(value, found))
        return found[0] + found[1]

    groups = [slice(place * HALF, (place + 1) * HALF) for place in range(ex_count)]
    row_lanes = ex_count * HALF
    middle = (left_ref.shape[1] + row_lanes) // 2
    blocks = [slice(row_lanes, middle), slice(middle, left_ref.shape[1])]
    rows = [picked(holder ^ step, groups) for step in range(1, ex_count)]
    return rows, picked(holder & 1, blocks)


def send_kernel(ex_count, left_ref, right_ref, send_ref):
    rows, columns = last_half(ex_count, lax.axis_index("tp") // 2 ^ 1, left_ref, right_ref)
    lanes = (ex_count - 1) * HALF
    send_ref[:, :lanes] = join(rows, 1)
    send_ref[:, lanes:] = columns


def last_sent(left, right, ex_count):
    row_lanes = ex_count * HALF
    shape = (left.shape[0], (left.shape[1] - row_lanes) // 2 + row_lanes - HALF)
    return call(
        functools.partial(send_kernel, ex_count),
        [(shape, jnp.float32)],
        [VMEM, VMEM],
        0.5,
        "last_sent",
    )(left, right)[0]


def pieces_kernel(ex_count, scaling, left_ref, right_ref, came_ref, _, *piece_refs):
    holder = lax.axis_index("tp") // 2
    rows, columns = last_half(ex_count, holder, left_ref, right_ref)
    rows = [
        ((row + came_ref[:, place * HALF : (place + 1) * HALF]) * scaling).astype(jnp.bfloat16)
        for place, row in enumerate(rows)
    ]
    columns = ((columns + came_ref[:, (ex_count - 1) * HALF :]) * scaling).astype(jnp.bfloat16)
    for step, ref in enumerate(piece_refs):
        distance = lax.axis_index("ex") ^ step ^ holder
        wanted = rows[0]
        for place in range(1, ex_count - 1):
            wanted = jnp.where(distance - 1 == place, rows[place], wanted)
        ref[:, :HALF] = wanted
        ref[:, HALF:] = columns


def pieces(left, right, came, ex_count, scaling, after):
    shape = (left.shape[0], came.shape[1] - (ex_count - 2) * HALF)
    return call(
        functools.partial(pieces_kernel, ex_count, scaling),
        [(shape, jnp.bfloat16)] * ex_count,
        [VMEM, VMEM, VMEM, ANYWHERE],
        0.5,
        "pieces",
    )(left, right, came, after)


def tdot(left, right):
    return lax.dot_general(left, right, (((0,), (0,)), ((), ())), preferred_element_type=jnp.float32)


def row_of(value, row):
    return jnp.broadcast_to(value[row : row + 1, :], value.shape)


def factor_stripe(rows_u, rows_z, offset):
    groups = len(rows_u)
    count = 8 * groups
    sub = lax.broadcasted_iota(jnp.int32, (8, BLOCK), 0)
    rows_u, rows_z = list(rows_u), list(rows_z)
    pivots = [jnp.ones((8, BLOCK), jnp.float32) for _ in range(groups)]

    def taken(base):
        return {
            c: {
                v: jnp.broadcast_to(rows_u[v][:, offset + c : offset + c + 1], (8, BLOCK))
                for v in range(c // 8, groups)
            }
            for c in range(base, base + SUB)
        }

    columns = taken(0)
    pivot = row_of(columns[0][0], 0)
    for j in range(count):
        g, s = divmod(j, 8)
        if j % SUB == SUB - LEAD and j + LEAD < count:
            columns.update(taken(j + LEAD))
        column = columns.pop(j)
        inverse = 1.0 / pivot
        pivots[g] = jnp.where(sub == s, pivot, pivots[g])
        if j + 1 < count:
            n, r = divmod(j + 1, 8)
            weight = row_of(column[n], r)
            following = columns[j + 1]
            pivot = row_of(following[n], r) - (weight * weight) * inverse
            for v in range(n, groups):
                following[v] = following[v] - (column[v] * weight) * inverse
        factors = {v: column[v] * inverse for v in range(g, groups)}
        for c, other in columns.items():
            if c > j + 1:
                weight = row_of(column[c // 8], c % 8)
                for v in range(c // 8, groups):
                    other[v] = other[v] - factors[v] * weight
        factors[g] = jnp.where(sub > s, factors[g], 0.0)
        row_u, row_z = row_of(rows_u[g], s), row_of(rows_z[g], s)
        for v in range(g + (s == 7), groups):
            rows_u[v] = rows_u[v] - factors[v] * row_u
            rows_z[v] = rows_z[v] - factors[v] * row_z
    scales = [lax.rsqrt(pivot) for pivot in pivots]
    return (
        [row * scale for row, scale in zip(rows_u, scales)],
        [row * scale for row, scale in zip(rows_z, scales)],
    )


def thirds(value):
    high = value.astype(jnp.bfloat16)
    rest = value - high.astype(jnp.float32)
    middle = rest.astype(jnp.bfloat16)
    return high, middle, (rest - middle.astype(jnp.float32)).astype(jnp.bfloat16)


def exact_dot(left, right, axes=(1, 0)):
    left_parts, right_parts = thirds(left), thirds(right)
    terms = ((0, 0), (0, 1), (1, 0), (0, 2), (2, 0), (1, 1))
    count = max(1, min(len(terms), DEPTH // left.shape[axes[0]]))
    total = None
    for start in range(0, len(terms), count):
        some = terms[start : start + count]
        term = lax.dot_general(
            join([left_parts[i] for i, _ in some], axes[0]),
            join([right_parts[j] for _, j in some], axes[1]),
            (((axes[0],), (axes[1],)), ((), ())),
            preferred_element_type=jnp.float32,
        )
        total = term if total is None else total + term
    return total


def identity_mask(shape):
    return lax.broadcasted_iota(jnp.int32, shape, 0) == lax.broadcasted_iota(jnp.int32, shape, 1)


def factor_start(block):
    unit = identity_mask(block.shape).astype(jnp.float32)
    return factor_step(block, unit, 0)


def factor_step(rest_u, rest_z, offset):
    groups = STRIPE // 8
    upper, inverse = factor_stripe(
        [rest_u[8 * v : 8 * v + 8] for v in range(groups)],
        [rest_z[8 * v : 8 * v + 8] for v in range(groups)],
        offset,
    )
    upper, inverse = jnp.concatenate(upper, axis=0), jnp.concatenate(inverse, axis=0)
    if offset + STRIPE == BLOCK:
        return inverse, None, None
    update = exact_dot(upper, jnp.concatenate([upper, inverse], axis=1), (0, 0))[offset + STRIPE :]
    return inverse, rest_u[STRIPE:] - update[:, :BLOCK], rest_z[STRIPE:] - update[:, BLOCK:]


def factor_end(inverse, rest_u, rest_z):
    done = [inverse]
    for offset in range(STRIPE, BLOCK, STRIPE):
        inverse, rest_u, rest_z = factor_step(rest_u, rest_z, offset)
        done.append(inverse)
    return jnp.concatenate(done, axis=0)


def in_pair_order(even, refs, lanes=slice(None)):
    values = [ref[:, lanes] for ref in refs]
    count = len(values) // 2
    mine, other = join(values[:count], 0), join(values[count:], 0)
    return join([jnp.where(even, mine, other), jnp.where(even, other, mine)], 0)


def eliminate(gram, turned, upper_refs, done_refs, rest_refs, started=None):
    square = (BLOCK, BLOCK)
    keep = lax.broadcasted_iota(jnp.int32, square, 0) <= lax.broadcasted_iota(jnp.int32, square, 1)
    block = gram[:BLOCK, :BLOCK]
    for index, (upper_ref, done_ref) in enumerate(zip(upper_refs, done_refs)):
        if index > 0 or started is None:
            started = factor_start(block)
        inverse = factor_end(*started)
        if index + 1 < len(upper_refs):
            beside = exact_dot(inverse, gram[:BLOCK, BLOCK : 2 * BLOCK])
            ahead = gram[BLOCK : 2 * BLOCK, BLOCK : 2 * BLOCK] - exact_dot(beside, beside, (0, 0))
        upper_ref[:, :BLOCK] = jnp.where(keep, exact_dot(inverse, block), 0.0)
        done = exact_dot(turned[:, :BLOCK], inverse, (1, 1))
        done_ref[...] = done
        if gram.shape[0] > BLOCK:
            rest = exact_dot(inverse, gram[:BLOCK, BLOCK:])
            upper_ref[:, BLOCK:] = rest
            gram = gram[BLOCK:, BLOCK:] - exact_dot(rest, rest, (0, 0))
            turned = turned[:, BLOCK:] - exact_dot(done, rest)
        if index + 1 < len(upper_refs):
            block = ahead
    if rest_refs:
        rest_refs[0][...] = gram
        rest_refs[1][...] = turned


def first_blocks_kernel(blocks, count, ridge_ref, *refs):
    phi_refs, out_refs = refs[:count], refs[count:]
    phi = in_pair_order(even_of_pair(), phi_refs)
    examples, width = phi.shape
    gram = tdot(phi, phi) * (1.0 / examples) + jnp.where(identity_mask((width, width)), ridge_ref[...], 0.0)
    eliminate(
        gram, phi.astype(jnp.float32), out_refs[:blocks], out_refs[blocks : 2 * blocks], out_refs[2 * blocks :]
    )


def start_block_kernel(block_ref, *out_refs):
    for ref, value in zip(out_refs, factor_start(block_ref[:BLOCK, :BLOCK])):
        ref[...] = value


def last_blocks_kernel(blocks, gram_ref, turned_ref, inverse_ref, rest_u_ref, rest_z_ref, *refs):
    started = (inverse_ref[...], rest_u_ref[...], rest_z_ref[...])
    eliminate(gram_ref[...], turned_ref[...], refs[:blocks], refs[blocks:], (), started)


def block_shapes(width, examples, blocks):
    rest = width - blocks * BLOCK
    shapes = [(BLOCK, width - index * BLOCK) for index in range(blocks)] + [(examples, BLOCK)] * blocks
    if rest:
        shapes += [(rest, rest), (examples, rest)]
    return [(shape, jnp.float32) for shape in shapes]


def taken_apart(results, blocks):
    return list(results[:blocks]), list(results[blocks : 2 * blocks]), results[2 * blocks :]


def first_blocks(ridge, phi, blocks):
    examples, width = sum(part.shape[0] for part in phi), phi[0].shape[1]
    results = call(
        functools.partial(first_blocks_kernel, blocks, len(phi)),
        block_shapes(width, examples, blocks),
        [VMEM] * (1 + len(phi)),
        3.5,
        "gram_first_blocks",
    )(ridge, *phi)
    return taken_apart(results, blocks)


def start_block(gram):
    shapes = [(STRIPE, BLOCK), (BLOCK - STRIPE, BLOCK), (BLOCK - STRIPE, BLOCK)]
    return call(
        start_block_kernel, [(shape, jnp.float32) for shape in shapes], [VMEM], 1.5, "start_block"
    )(gram)


def last_blocks(rest, started):
    gram, turned = rest
    blocks = gram.shape[0] // BLOCK
    results = call(
        functools.partial(last_blocks_kernel, blocks),
        block_shapes(gram.shape[0], turned.shape[0], blocks),
        [VMEM] * (2 + len(started)),
        4.5,
        "last_blocks",
    )(gram, turned, *started)
    return taken_apart(results, blocks)


def assembled_columns(refs, height, width):
    return join([ref[:, start : start + width] for start in (height, height + width) for ref in refs], 0)


def lower(uppers, row, lane):
    if row < lane:
        return jnp.zeros((BLOCK, BLOCK), jnp.float32)
    return uppers[lane // BLOCK][:, row - lane : row - lane + BLOCK].T


def put_lower(uppers, ref, first):
    for row in range(0, ref.shape[0], BLOCK):
        for lane in range(0, ref.shape[1], BLOCK):
            ref[row : row + BLOCK, lane : lane + BLOCK] = lower(uppers, first + row, lane)


def solve(features, parts_ref):
    turned = features.T
    product = jnp.dot(join([turned] * 3, 1), parts_ref[...], preferred_element_type=jnp.float32)
    return turned, product * (1.0 / features.shape[0])


def column_kernel(blocks, count, height, *refs):
    uppers, dones = refs[:blocks], refs[blocks : 2 * blocks]
    phi_refs, mine = refs[2 * blocks : 2 * blocks + count], refs[2 * blocks + count : -6]
    columns_ref, parts_ref, *third_refs, solved_ref = refs[-6:]
    width = columns_ref.shape[1]
    column_block = lax.axis_index("tp")
    phi = in_pair_order(even_of_pair(), phi_refs)
    columns = jnp.where(column_block == 0, phi, assembled_columns(mine, height, width))
    columns_ref[...] = columns
    parts_ref[...] = join(list(thirds(join([ref[...] for ref in dones], 1))), 0)
    solved_ref[...] = solve(columns, parts_ref)[1]
    pl.when(column_block == 0)(functools.partial(put_lower, uppers, solved_ref, 0))
    for ref, part in zip(third_refs, thirds(solved_ref[...])):
        ref[...] = part


def columns_solved(uppers, dones, phi, mine, height, width):
    panel, examples = uppers[0].shape[1], sum(part.shape[0] for part in phi)
    operands = [*uppers, *dones, *phi, *mine]
    shapes = [(examples, width), (3 * examples, panel)] + [(width, panel)] * 3
    return call(
        functools.partial(column_kernel, len(uppers), len(phi), height),
        [(shape, jnp.bfloat16) for shape in shapes],
        [VMEM] * len(operands),
        1,
        "columns_solved",
        [pltpu.VMEM((width, panel), jnp.float32)],
        vmem=24,
    )(*operands)


def finish_kernel(blocks, count, blk_count, ridge_ref, columns_ref, parts_ref, *refs):
    solved, refs = [ref[...] for ref in refs[:3]], refs[3:]
    uppers = refs[:blocks]
    phi_refs, piece_refs = refs[blocks : blocks + count], refs[blocks + count : -2]
    panel_ref, trailing_ref = refs[-2:]
    height, panel = panel_ref.shape
    width = trailing_ref.shape[1]
    even = even_of_pair()
    ex_index, column_block, blk_index = (lax.axis_index(axis) for axis in ("ex", "tp", "blk"))
    row_group = ex_index * blk_count + blk_index
    phi = in_pair_order(even, phi_refs)
    rows = in_pair_order(even, piece_refs, slice(0, height))
    columns = columns_ref[...]
    pair_columns = assembled_columns(piece_refs[count // 2 :], height, width)
    groups = width // height
    held = jnp.where(blk_index // groups == column_block % 2, columns, pair_columns)
    for place in range(groups):
        inside = (ex_index == column_block // 2) & (blk_index % groups == place)
        rows = jnp.where(inside, held[:, place * height : (place + 1) * height], rows)
    for start in range(0, panel, height):
        rows = jnp.where(row_group * height == start, phi[:, start : start + height], rows)
    turned, panel_ref[...] = solve(rows, parts_ref)
    for group in range(panel // height):
        pl.when(row_group == group)(functools.partial(put_lower, uppers, panel_ref, group * height))
    shape = (height, width)
    diagonal = row_group * height + lax.broadcasted_iota(
        jnp.int32, shape, 0
    ) == column_block * width + lax.broadcasted_iota(jnp.int32, shape, 1)
    gram = jnp.dot(turned, columns, preferred_element_type=jnp.float32) * (1.0 / columns.shape[0])
    total = gram + jnp.where(diagonal, ridge_ref[...], 0.0)
    for left, right in zip(*term_parts(thirds(panel_ref[...]), solved)):
        total = total - lax.dot_general(
            left, right, (((1,), (1,)), ((), ())), preferred_element_type=jnp.float32
        )
    trailing_ref[...] = total


def term_parts(left_parts, right_parts):
    terms = ((0, 0), (0, 1), (1, 0), (0, 2), (2, 0), (1, 1))
    return [left_parts[i] for i, _ in terms], [right_parts[j] for _, j in terms]


def finish(ridge, uppers, dones, phi, gathered, height, width, blk_count):
    panel = uppers[0].shape[1]
    mine = gathered[: len(gathered) // 2]
    solved = columns_solved(uppers, dones, phi, mine, height, width)
    operands = [*solved, *uppers, *phi, *gathered]
    return call(
        functools.partial(finish_kernel, len(uppers), len(phi), blk_count),
        [((height, panel), jnp.float32), ((height, width), jnp.float32)],
        [VMEM] * (1 + len(operands)),
        2,
        "finish",
        vmem=24,
    )(ridge, *operands)


def swapped(value, axis, bit):
    return lax.ppermute(value, axis, [(s, s ^ bit) for s in range(lax.axis_size(axis))])


def ex_parts(own):
    return [own[0]] + [swapped(own[step], "ex", step) for step in range(1, lax.axis_size("ex"))]


def with_pair(parts):
    return list(parts) + [swapped(part, "tp", 1) for part in parts]


def shards(gradients, selection, seed_value, ridge_value):
    ex_count = lax.axis_size("ex")
    tp_count = lax.axis_size("tp")
    blk_count = lax.axis_size("blk")
    coord_dev = gradients.shape[1]
    column_width = HALF * ex_count * blk_count // tp_count
    scaling = 1.0 / math.sqrt(coord_dev * tp_count)
    seed, ridge = seed_value.reshape(1, 1), ridge_value.reshape(1, 1)

    mine, theirs, chosen = panel_part(seed, selection, gradients)
    total = mine + swapped(theirs, "tp", 1)
    halves = total
    bit = 2
    while bit < tp_count:
        total = total + swapped(total, "tp", bit)
        bit *= 2
    phi = ex_parts([(total * scaling).astype(jnp.bfloat16)] * ex_count)

    first = blocks_part(seed, chosen, range(1, 1 + tp_count // 2), column_width, halves)
    left, right = other_parts(seed, chosen, first, tp_count, blk_count, total)
    phi[1:], right = lax.optimization_barrier((phi[1:], right))
    right = swapped(right, "tp", 1)
    bit = tp_count // 2
    while bit > 2:
        left, right = halve(left, right, ex_count, bit)
        right = swapped(right, "tp", bit)
        bit //= 2
    came = swapped(last_sent(left, right, ex_count), "tp", 2)

    phi = with_pair(phi)
    half = PANEL // BLOCK // 2
    uppers, dones, rest = first_blocks(ridge, phi, half)
    started = start_block(rest[0])
    gathered = pieces(left, right, came, ex_count, scaling, started[0])
    other = swapped(gathered[0], "tp", 1)
    gathered = ex_parts(gathered)
    started, other = lax.optimization_barrier((started, other))
    more_uppers, more_dones, _ = last_blocks(rest, started)
    gathered[1:], more_dones = lax.optimization_barrier((gathered[1:], more_dones))
    gathered = [*gathered, other, *(swapped(part, "tp", 1) for part in gathered[1:])]
    uppers, dones = uppers + more_uppers, dones + more_dones
    return tuple(finish(ridge, uppers, dones, phi, gathered, HALF, column_width, blk_count))


def solution(mesh):
    in_specs = (P("ex", "tp"), P("ex"), P(), P())
    out_specs = (P(("ex", "blk"), None), P(("ex", "blk"), "tp"))
    return jax.shard_map(shards, mesh=mesh, in_specs=in_specs, out_specs=out_specs, check_vma=False)
```

```python
import functools
import math

import jax
import jax.numpy as jnp
from jax import lax
from jax.experimental import pallas as pl
from jax.experimental.pallas import tpu as pltpu
from jax.sharding import PartitionSpec as P

PANEL = 512
HALF = 256
STRIPE = 64
SUB = 8
LEAD = 3
BLOCK = 128
DEPTH = 256
SEGMENT = 128
VMEM = pl.BlockSpec(memory_space=pltpu.VMEM)
SMEM = pl.BlockSpec(memory_space=pltpu.SMEM)
ANYWHERE = pl.BlockSpec(memory_space=pl.ANY)


def call(kernel, out_shape, in_specs, microseconds, name, scratch=(), vmem=16):
    shapes = [jax.ShapeDtypeStruct(shape, dtype) for shape, dtype in out_shape]
    return pl.pallas_call(
        kernel,
        out_shape=shapes,
        in_specs=in_specs,
        out_specs=[VMEM] * len(shapes),
        scratch_shapes=list(scratch),
        compiler_params=pltpu.CompilerParams(vmem_limit_bytes=vmem * 1024 * 1024),
        cost_estimate=pl.CostEstimate(
            flops=int(microseconds * 1_100_000_000), bytes_accessed=1_000_000, transcendentals=0
        ),
        name=name,
    )


def join(parts, axis):
    return parts[0] if len(parts) == 1 else jnp.concatenate(parts, axis)


def shifted(value, amount):
    return lax.shift_right_logical(value, jnp.full_like(value, amount))


def sign_tile(seed_word, coordinate, feature, shape):
    rows = (lax.broadcasted_iota(jnp.int32, (shape[0], 1), 0) + coordinate) * jnp.int32(-1640531535)
    columns = (lax.broadcasted_iota(jnp.int32, (1, shape[1]), 1) + feature) * jnp.int32(668265263) + seed_word
    hashed = rows + columns
    hashed = (hashed ^ shifted(hashed, 16)) * jnp.int32(-2048144789)
    hashed = (hashed ^ shifted(hashed, 13)) * jnp.int32(-1028477387)
    decided = (hashed ^ shifted(hashed, 16)).astype(jnp.int16) & jnp.int16(128)
    return jnp.where(decided == 0, jnp.bfloat16(1.0), jnp.bfloat16(-1.0))


def segment_signs(seed_ref, coordinates, feature, width, index):
    first = lax.axis_index("tp") * coordinates + index * SEGMENT
    seed = seed_ref[0] if len(seed_ref.shape) == 1 else seed_ref[...]
    return sign_tile(seed, first, feature, (SEGMENT, width))


def project_step(seed_ref, chosen_ref, feature, width, index, total):
    start = pl.multiple_of(index * SEGMENT, SEGMENT)
    signs = segment_signs(seed_ref, chosen_ref.shape[1], feature, width, index)
    return total + jnp.dot(chosen_ref[:, pl.ds(start, SEGMENT)], signs, preferred_element_type=jnp.float32)


def project_tile(seed_ref, chosen_ref, feature, width, unroll):
    rows, coordinates = chosen_ref.shape
    step = functools.partial(project_step, seed_ref, chosen_ref, feature, width)
    zero = jnp.zeros((rows, width), jnp.float32)
    return lax.fori_loop(0, coordinates // SEGMENT, step, zero, unroll=unroll)


def even_of_pair():
    return lax.axis_index("tp") % 2 == 0


def panel_signs_kernel(seed_ref, signs_ref):
    coordinates, width = signs_ref.shape
    for step in range(coordinates // SEGMENT):
        signs_ref[step * SEGMENT : (step + 1) * SEGMENT, :] = segment_signs(
            seed_ref, coordinates, 0, width, step
        )


def panel_signs(seed, coordinates):
    return call(
        panel_signs_kernel, [((coordinates, PANEL), jnp.bfloat16)], [SMEM], 2, "panel_signs"
    )(seed)[0]


def panel_part_kernel(selection_ref, pool_ref, signs_ref, mine_ref, theirs_ref, chosen_ref):
    half = mine_ref.shape[0]
    shape = (pool_ref.shape[0], chosen_ref.shape[0])
    picked = jnp.where(lax.broadcasted_iota(jnp.int32, shape, 0) == selection_ref[...], 1.0, 0.0)
    chosen = tdot(picked.astype(jnp.bfloat16), pool_ref[...]).astype(jnp.bfloat16)
    chosen_ref[...] = chosen
    total = jnp.dot(chosen, signs_ref[...], preferred_element_type=jnp.float32)
    even = even_of_pair()
    mine_ref[...] = jnp.where(even, total[:half], total[half:])
    theirs_ref[...] = jnp.where(even, total[half:], total[:half])


def panel_part(seed, selection, pool):
    rows, coordinates = selection.shape[0], pool.shape[1]
    return call(
        panel_part_kernel,
        [((rows // 2, PANEL), jnp.float32)] * 2 + [((rows, coordinates), jnp.bfloat16)],
        [VMEM, VMEM, VMEM],
        1,
        "panel_part",
    )(selection[None, :], pool, panel_signs(seed.reshape(-1), coordinates))


def blocks_part_kernel(blocks, seed_ref, chosen_ref, _, *part_refs):
    width = part_refs[0].shape[1]
    for block, part_ref in zip(blocks, part_refs):
        part_ref[...] = project_tile(seed_ref, chosen_ref, block * width, width, len(blocks) <= 2)


def blocks_part(seed, chosen, blocks, width, after):
    return call(
        functools.partial(blocks_part_kernel, blocks),
        [((chosen.shape[0], width), jnp.float32)] * len(blocks),
        [VMEM, VMEM, ANYWHERE],
        2 * len(blocks),
        "blocks_part",
        vmem=32 if len(blocks) > 2 else 16,
    )(seed, chosen, after)


def other_parts_kernel(tp_count, blk_count, seed_ref, chosen_ref, _, *refs):
    *first_refs, mine_ref, theirs_ref = refs
    rows = chosen_ref.shape[0]
    half = rows // 2
    width = first_refs[0].shape[1]
    groups = width // HALF
    row_lanes = tp_count * groups // blk_count * HALF
    even = even_of_pair()
    for ref in (mine_ref, theirs_ref):
        ref[:, : row_lanes + 2 * width] = jnp.zeros((half, row_lanes + 2 * width), jnp.float32)

    def place(ref, lane, part):
        ref[:, lane : lane + width] = part[:half]
        ref[:, lane + width : lane + 2 * width] = part[half:]

    for block in range(1, tp_count):
        lane = row_lanes + block // 2 * 2 * width
        if block <= len(first_refs):
            part = first_refs[block - 1][...]
        else:
            part = project_tile(seed_ref, chosen_ref, block * width, width, tp_count <= 4)
        own = lax.axis_index("tp") % 2 == block % 2
        pl.when(own)(functools.partial(place, mine_ref, lane, part))
        pl.when(jnp.logical_not(own))(functools.partial(place, theirs_ref, lane, part))
        for which in range(groups):
            group = block * groups + which

            @pl.when(lax.axis_index("blk") == group % blk_count)
            def _(part=part[:, which * HALF : (which + 1) * HALF], lane=group // blk_count * HALF):
                mine_ref[:, lane : lane + HALF] = jnp.where(even, part[:half], part[half:])
                theirs_ref[:, lane : lane + HALF] = jnp.where(even, part[half:], part[:half])


def other_parts(seed, chosen, first, tp_count, blk_count, after):
    rows, width = first[0].shape
    lanes = tp_count * (width // HALF) // blk_count * HALF + tp_count // 2 * 2 * width
    return call(
        functools.partial(other_parts_kernel, tp_count, blk_count),
        [((rows // 2, lanes), jnp.float32)] * 2,
        [VMEM, VMEM, ANYWHERE] + [VMEM] * len(first),
        2 * (tp_count - 1 - len(first)),
        "other_parts",
        vmem=16 if tp_count <= 4 else 48,
    )(seed, chosen, after, *first)


def group_at(rows, index, count):
    found = rows[:, :HALF]
    for place in range(1, count):
        found = jnp.where(index == place, rows[:, place * HALF : (place + 1) * HALF], found)
    return found


def halve_kernel(ex_count, bit, left_ref, right_ref, keep_ref, send_ref):
    row_lanes = ex_count * HALF
    upper = lax.axis_index("tp") & bit != 0
    total = left_ref[...] + right_ref[...]
    middle = (total.shape[1] + row_lanes) // 2
    keep_ref[:, :row_lanes] = total[:, :row_lanes]
    send_ref[:, :row_lanes] = total[:, :row_lanes]
    keep_ref[:, row_lanes:] = jnp.where(upper, total[:, middle:], total[:, row_lanes:middle])
    send_ref[:, row_lanes:] = jnp.where(upper, total[:, row_lanes:middle], total[:, middle:])


def halve(left, right, ex_count, bit):
    shape = (left.shape[0], (left.shape[1] + ex_count * HALF) // 2)
    return call(
        functools.partial(halve_kernel, ex_count, bit),
        [(shape, jnp.float32)] * 2,
        [VMEM, VMEM],
        0.5,
        "halve",
    )(left, right)


def last_half(ex_count, holder, left_ref, right_ref):
    def picked(index, places):
        found = None
        for place, lanes in enumerate(places):
            value = (left_ref[:, lanes], right_ref[:, lanes])
            if found is None:
                found = value
            else:
                found = tuple(jnp.where(index == place, new, old) for new, old in zip(value, found))
        return found[0] + found[1]

    groups = [slice(place * HALF, (place + 1) * HALF) for place in range(ex_count)]
    row_lanes = ex_count * HALF
    middle = (left_ref.shape[1] + row_lanes) // 2
    blocks = [slice(row_lanes, middle), slice(middle, left_ref.shape[1])]
    rows = [picked(holder ^ step, groups) for step in range(1, ex_count)]
    return rows, picked(holder & 1, blocks)


def send_kernel(ex_count, left_ref, right_ref, send_ref):
    rows, columns = last_half(ex_count, lax.axis_index("tp") // 2 ^ 1, left_ref, right_ref)
    lanes = (ex_count - 1) * HALF
    send_ref[:, :lanes] = join(rows, 1)
    send_ref[:, lanes:] = columns


def last_sent(left, right, ex_count):
    row_lanes = ex_count * HALF
    shape = (left.shape[0], (left.shape[1] - row_lanes) // 2 + row_lanes - HALF)
    return call(
        functools.partial(send_kernel, ex_count),
        [(shape, jnp.float32)],
        [VMEM, VMEM],
        0.5,
        "last_sent",
    )(left, right)[0]


def pieces_kernel(ex_count, scaling, left_ref, right_ref, came_ref, _, *piece_refs):
    holder = lax.axis_index("tp") // 2
    rows, columns = last_half(ex_count, holder, left_ref, right_ref)
    rows = [
        ((row + came_ref[:, place * HALF : (place + 1) * HALF]) * scaling).astype(jnp.bfloat16)
        for place, row in enumerate(rows)
    ]
    columns = ((columns + came_ref[:, (ex_count - 1) * HALF :]) * scaling).astype(jnp.bfloat16)
    for step, ref in enumerate(piece_refs):
        distance = lax.axis_index("ex") ^ step ^ holder
        wanted = rows[0]
        for place in range(1, ex_count - 1):
            wanted = jnp.where(distance - 1 == place, rows[place], wanted)
        ref[:, :HALF] = wanted
        ref[:, HALF:] = columns


def pieces(left, right, came, ex_count, scaling, after):
    shape = (left.shape[0], came.shape[1] - (ex_count - 2) * HALF)
    return call(
        functools.partial(pieces_kernel, ex_count, scaling),
        [(shape, jnp.bfloat16)] * ex_count,
        [VMEM, VMEM, VMEM, ANYWHERE],
        0.5,
        "pieces",
    )(left, right, came, after)


def tdot(left, right):
    return lax.dot_general(left, right, (((0,), (0,)), ((), ())), preferred_element_type=jnp.float32)


def row_of(value, row):
    return jnp.broadcast_to(value[row : row + 1, :], value.shape)


def factor_stripe(rows_u, rows_z, offset):
    groups = len(rows_u)
    count = 8 * groups
    sub = lax.broadcasted_iota(jnp.int32, (8, BLOCK), 0)
    rows_u, rows_z = list(rows_u), list(rows_z)
    pivots = [jnp.ones((8, BLOCK), jnp.float32) for _ in range(groups)]

    def taken(base):
        return {
            c: {
                v: jnp.broadcast_to(rows_u[v][:, offset + c : offset + c + 1], (8, BLOCK))
                for v in range(c // 8, groups)
            }
            for c in range(base, base + SUB)
        }

    columns = taken(0)
    pivot = row_of(columns[0][0], 0)
    for j in range(count):
        g, s = divmod(j, 8)
        if j % SUB == SUB - LEAD and j + LEAD < count:
            columns.update(taken(j + LEAD))
        column = columns.pop(j)
        inverse = 1.0 / pivot
        pivots[g] = jnp.where(sub == s, pivot, pivots[g])
        if j + 1 < count:
            n, r = divmod(j + 1, 8)
            weight = row_of(column[n], r)
            following = columns[j + 1]
            pivot = row_of(following[n], r) - (weight * weight) * inverse
            for v in range(n, groups):
                following[v] = following[v] - (column[v] * weight) * inverse
        factors = {v: column[v] * inverse for v in range(g, groups)}
        for c, other in columns.items():
            if c > j + 1:
                weight = row_of(column[c // 8], c % 8)
                for v in range(c // 8, groups):
                    other[v] = other[v] - factors[v] * weight
        factors[g] = jnp.where(sub > s, factors[g], 0.0)
        row_u, row_z = row_of(rows_u[g], s), row_of(rows_z[g], s)
        for v in range(g + (s == 7), groups):
            rows_u[v] = rows_u[v] - factors[v] * row_u
            rows_z[v] = rows_z[v] - factors[v] * row_z
    scales = [lax.rsqrt(pivot) for pivot in pivots]
    return (
        [row * scale for row, scale in zip(rows_u, scales)],
        [row * scale for row, scale in zip(rows_z, scales)],
    )


def thirds(value):
    high = value.astype(jnp.bfloat16)
    rest = value - high.astype(jnp.float32)
    middle = rest.astype(jnp.bfloat16)
    return high, middle, (rest - middle.astype(jnp.float32)).astype(jnp.bfloat16)


def exact_dot(left, right, axes=(1, 0)):
    left_parts, right_parts = thirds(left), thirds(right)
    terms = ((0, 0), (0, 1), (1, 0), (0, 2), (2, 0), (1, 1))
    count = max(1, min(len(terms), DEPTH // left.shape[axes[0]]))
    total = None
    for start in range(0, len(terms), count):
        some = terms[start : start + count]
        term = lax.dot_general(
            join([left_parts[i] for i, _ in some], axes[0]),
            join([right_parts[j] for _, j in some], axes[1]),
            (((axes[0],), (axes[1],)), ((), ())),
            preferred_element_type=jnp.float32,
        )
        total = term if total is None else total + term
    return total


def identity_mask(shape):
    return lax.broadcasted_iota(jnp.int32, shape, 0) == lax.broadcasted_iota(jnp.int32, shape, 1)


def factor_start(block):
    unit = identity_mask(block.shape).astype(jnp.float32)
    return factor_step(block, unit, 0)


def factor_step(rest_u, rest_z, offset):
    groups = STRIPE // 8
    upper, inverse = factor_stripe(
        [rest_u[8 * v : 8 * v + 8] for v in range(groups)],
        [rest_z[8 * v : 8 * v + 8] for v in range(groups)],
        offset,
    )
    upper, inverse = jnp.concatenate(upper, axis=0), jnp.concatenate(inverse, axis=0)
    if offset + STRIPE == BLOCK:
        return inverse, None, None
    update = exact_dot(upper, jnp.concatenate([upper, inverse], axis=1), (0, 0))[offset + STRIPE :]
    return inverse, rest_u[STRIPE:] - update[:, :BLOCK], rest_z[STRIPE:] - update[:, BLOCK:]


def factor_end(inverse, rest_u, rest_z):
    done = [inverse]
    for offset in range(STRIPE, BLOCK, STRIPE):
        inverse, rest_u, rest_z = factor_step(rest_u, rest_z, offset)
        done.append(inverse)
    return jnp.concatenate(done, axis=0)


def in_pair_order(even, refs, lanes=slice(None)):
    values = [ref[:, lanes] for ref in refs]
    count = len(values) // 2
    mine, other = join(values[:count], 0), join(values[count:], 0)
    return join([jnp.where(even, mine, other), jnp.where(even, other, mine)], 0)


def eliminate(gram, turned, upper_refs, done_refs, rest_refs, started=None):
    square = (BLOCK, BLOCK)
    keep = lax.broadcasted_iota(jnp.int32, square, 0) <= lax.broadcasted_iota(jnp.int32, square, 1)
    block = gram[:BLOCK, :BLOCK]
    for index, (upper_ref, done_ref) in enumerate(zip(upper_refs, done_refs)):
        if index > 0 or started is None:
            started = factor_start(block)
        inverse = factor_end(*started)
        if index + 1 < len(upper_refs):
            beside = exact_dot(inverse, gram[:BLOCK, BLOCK : 2 * BLOCK])
            ahead = gram[BLOCK : 2 * BLOCK, BLOCK : 2 * BLOCK] - exact_dot(beside, beside, (0, 0))
        upper_ref[:, :BLOCK] = jnp.where(keep, exact_dot(inverse, block), 0.0)
        done = exact_dot(turned[:, :BLOCK], inverse, (1, 1))
        done_ref[...] = done
        if gram.shape[0] > BLOCK:
            rest = exact_dot(inverse, gram[:BLOCK, BLOCK:])
            upper_ref[:, BLOCK:] = rest
            gram = gram[BLOCK:, BLOCK:] - exact_dot(rest, rest, (0, 0))
            turned = turned[:, BLOCK:] - exact_dot(done, rest)
        if index + 1 < len(upper_refs):
            block = ahead
    if rest_refs:
        rest_refs[0][...] = gram
        rest_refs[1][...] = turned


def first_blocks_kernel(blocks, count, ridge_ref, *refs):
    phi_refs, out_refs = refs[:count], refs[count:]
    phi = in_pair_order(even_of_pair(), phi_refs)
    examples, width = phi.shape
    gram = tdot(phi, phi) * (1.0 / examples) + jnp.where(identity_mask((width, width)), ridge_ref[...], 0.0)
    eliminate(
        gram, phi.astype(jnp.float32), out_refs[:blocks], out_refs[blocks : 2 * blocks], out_refs[2 * blocks :]
    )


def start_block_kernel(block_ref, *out_refs):
    for ref, value in zip(out_refs, factor_start(block_ref[:BLOCK, :BLOCK])):
        ref[...] = value


def last_blocks_kernel(blocks, gram_ref, turned_ref, inverse_ref, rest_u_ref, rest_z_ref, *refs):
    started = (inverse_ref[...], rest_u_ref[...], rest_z_ref[...])
    eliminate(gram_ref[...], turned_ref[...], refs[:blocks], refs[blocks:], (), started)


def block_shapes(width, examples, blocks):
    rest = width - blocks * BLOCK
    shapes = [(BLOCK, width - index * BLOCK) for index in range(blocks)] + [(examples, BLOCK)] * blocks
    if rest:
        shapes += [(rest, rest), (examples, rest)]
    return [(shape, jnp.float32) for shape in shapes]


def taken_apart(results, blocks):
    return list(results[:blocks]), list(results[blocks : 2 * blocks]), results[2 * blocks :]


def first_blocks(ridge, phi, blocks):
    examples, width = sum(part.shape[0] for part in phi), phi[0].shape[1]
    results = call(
        functools.partial(first_blocks_kernel, blocks, len(phi)),
        block_shapes(width, examples, blocks),
        [VMEM] * (1 + len(phi)),
        3.5,
        "gram_first_blocks",
    )(ridge, *phi)
    return taken_apart(results, blocks)


def start_block(gram):
    shapes = [(STRIPE, BLOCK), (BLOCK - STRIPE, BLOCK), (BLOCK - STRIPE, BLOCK)]
    return call(
        start_block_kernel, [(shape, jnp.float32) for shape in shapes], [VMEM], 1.5, "start_block"
    )(gram)


def last_blocks(rest, started):
    gram, turned = rest
    blocks = gram.shape[0] // BLOCK
    results = call(
        functools.partial(last_blocks_kernel, blocks),
        block_shapes(gram.shape[0], turned.shape[0], blocks),
        [VMEM] * (2 + len(started)),
        4.5,
        "last_blocks",
    )(gram, turned, *started)
    return taken_apart(results, blocks)


def assembled_columns(refs, height, width):
    return join([ref[:, start : start + width] for start in (height, height + width) for ref in refs], 0)


def lower(uppers, row, lane):
    if row < lane:
        return jnp.zeros((BLOCK, BLOCK), jnp.float32)
    return uppers[lane // BLOCK][:, row - lane : row - lane + BLOCK].T


def put_lower(uppers, ref, first):
    for row in range(0, ref.shape[0], BLOCK):
        for lane in range(0, ref.shape[1], BLOCK):
            ref[row : row + BLOCK, lane : lane + BLOCK] = lower(uppers, first + row, lane)


def solve(features, parts_ref):
    turned = features.T
    product = jnp.dot(join([turned] * 3, 1), parts_ref[...], preferred_element_type=jnp.float32)
    return turned, product * (1.0 / features.shape[0])


def column_kernel(blocks, count, height, *refs):
    uppers, dones = refs[:blocks], refs[blocks : 2 * blocks]
    phi_refs, mine = refs[2 * blocks : 2 * blocks + count], refs[2 * blocks + count : -6]
    columns_ref, parts_ref, *third_refs, solved_ref = refs[-6:]
    width = columns_ref.shape[1]
    column_block = lax.axis_index("tp")
    phi = in_pair_order(even_of_pair(), phi_refs)
    columns = jnp.where(column_block == 0, phi, assembled_columns(mine, height, width))
    columns_ref[...] = columns
    parts_ref[...] = join(list(thirds(join([ref[...] for ref in dones], 1))), 0)
    solved_ref[...] = solve(columns, parts_ref)[1]
    pl.when(column_block == 0)(functools.partial(put_lower, uppers, solved_ref, 0))
    for ref, part in zip(third_refs, thirds(solved_ref[...])):
        ref[...] = part


def columns_solved(uppers, dones, phi, mine, height, width):
    panel, examples = uppers[0].shape[1], sum(part.shape[0] for part in phi)
    operands = [*uppers, *dones, *phi, *mine]
    shapes = [(examples, width), (3 * examples, panel)] + [(width, panel)] * 3
    return call(
        functools.partial(column_kernel, len(uppers), len(phi), height),
        [(shape, jnp.bfloat16) for shape in shapes],
        [VMEM] * len(operands),
        1,
        "columns_solved",
        [pltpu.VMEM((width, panel), jnp.float32)],
        vmem=24,
    )(*operands)


def finish_kernel(blocks, count, blk_count, ridge_ref, columns_ref, parts_ref, *refs):
    solved, refs = [ref[...] for ref in refs[:3]], refs[3:]
    uppers = refs[:blocks]
    phi_refs, piece_refs = refs[blocks : blocks + count], refs[blocks + count : -2]
    panel_ref, trailing_ref = refs[-2:]
    height, panel = panel_ref.shape
    width = trailing_ref.shape[1]
    even = even_of_pair()
    ex_index, column_block, blk_index = (lax.axis_index(axis) for axis in ("ex", "tp", "blk"))
    row_group = ex_index * blk_count + blk_index
    phi = in_pair_order(even, phi_refs)
    rows = in_pair_order(even, piece_refs, slice(0, height))
    columns = columns_ref[...]
    pair_columns = assembled_columns(piece_refs[count // 2 :], height, width)
    groups = width // height
    held = jnp.where(blk_index // groups == column_block % 2, columns, pair_columns)
    for place in range(groups):
        inside = (ex_index == column_block // 2) & (blk_index % groups == place)
        rows = jnp.where(inside, held[:, place * height : (place + 1) * height], rows)
    for start in range(0, panel, height):
        rows = jnp.where(row_group * height == start, phi[:, start : start + height], rows)
    turned, panel_ref[...] = solve(rows, parts_ref)
    for group in range(panel // height):
        pl.when(row_group == group)(functools.partial(put_lower, uppers, panel_ref, group * height))
    shape = (height, width)
    diagonal = row_group * height + lax.broadcasted_iota(
        jnp.int32, shape, 0
    ) == column_block * width + lax.broadcasted_iota(jnp.int32, shape, 1)
    gram = jnp.dot(turned, columns, preferred_element_type=jnp.float32) * (1.0 / columns.shape[0])
    total = gram + jnp.where(diagonal, ridge_ref[...], 0.0)
    for left, right in zip(*term_parts(thirds(panel_ref[...]), solved)):
        total = total - lax.dot_general(
            left, right, (((1,), (1,)), ((), ())), preferred_element_type=jnp.float32
        )
    trailing_ref[...] = total


def term_parts(left_parts, right_parts):
    terms = ((0, 0), (0, 1), (1, 0), (0, 2), (2, 0), (1, 1))
    return [left_parts[i] for i, _ in terms], [right_parts[j] for _, j in terms]


def finish(ridge, uppers, dones, phi, gathered, height, width, blk_count):
    panel = uppers[0].shape[1]
    mine = gathered[: len(gathered) // 2]
    solved = columns_solved(uppers, dones, phi, mine, height, width)
    operands = [*solved, *uppers, *phi, *gathered]
    return call(
        functools.partial(finish_kernel, len(uppers), len(phi), blk_count),
        [((height, panel), jnp.float32), ((height, width), jnp.float32)],
        [VMEM] * (1 + len(operands)),
        2,
        "finish",
        vmem=24,
    )(ridge, *operands)


def swapped(value, axis, bit):
    return lax.ppermute(value, axis, [(s, s ^ bit) for s in range(lax.axis_size(axis))])


def ex_parts(own):
    return [own[0]] + [swapped(own[step], "ex", step) for step in range(1, lax.axis_size("ex"))]


def with_pair(parts):
    return list(parts) + [swapped(part, "tp", 1) for part in parts]


def shards(gradients, selection, seed_value, ridge_value):
    ex_count = lax.axis_size("ex")
    tp_count = lax.axis_size("tp")
    blk_count = lax.axis_size("blk")
    coord_dev = gradients.shape[1]
    column_width = HALF * ex_count * blk_count // tp_count
    scaling = 1.0 / math.sqrt(coord_dev * tp_count)
    seed, ridge = seed_value.reshape(1, 1), ridge_value.reshape(1, 1)

    mine, theirs, chosen = panel_part(seed, selection, gradients)
    total = mine + swapped(theirs, "tp", 1)
    halves = total
    bit = 2
    while bit < tp_count:
        total = total + swapped(total, "tp", bit)
        bit *= 2
    phi = ex_parts([(total * scaling).astype(jnp.bfloat16)] * ex_count)

    first = blocks_part(seed, chosen, range(1, 1 + tp_count // 2), column_width, halves)
    left, right = other_parts(seed, chosen, first, tp_count, blk_count, total)
    phi[1:], right = lax.optimization_barrier((phi[1:], right))
    right = swapped(right, "tp", 1)
    bit = tp_count // 2
    while bit > 2:
        left, right = halve(left, right, ex_count, bit)
        right = swapped(right, "tp", bit)
        bit //= 2
    came = swapped(last_sent(left, right, ex_count), "tp", 2)

    phi = with_pair(phi)
    half = PANEL // BLOCK // 2
    uppers, dones, rest = first_blocks(ridge, phi, half)
    started = start_block(rest[0])
    gathered = pieces(left, right, came, ex_count, scaling, started[0])
    other = swapped(gathered[0], "tp", 1)
    gathered = ex_parts(gathered)
    started, other = lax.optimization_barrier((started, other))
    more_uppers, more_dones, _ = last_blocks(rest, started)
    gathered[1:], more_dones = lax.optimization_barrier((gathered[1:], more_dones))
    gathered = [*gathered, other, *(swapped(part, "tp", 1) for part in gathered[1:])]
    uppers, dones = uppers + more_uppers, dones + more_dones
    return tuple(finish(ridge, uppers, dones, phi, gathered, HALF, column_width, blk_count))


def solution(mesh):
    in_specs = (P("ex", "tp"), P("ex"), P(), P())
    out_specs = (P(("ex", "blk"), None), P(("ex", "blk"), "tp"))
    return jax.shard_map(shards, mesh=mesh, in_specs=in_specs, out_specs=out_specs, check_vma=False)
```

```python
import functools
import math

import jax
import jax.numpy as jnp
from jax import lax
from jax.experimental import pallas as pl
from jax.experimental.pallas import tpu as pltpu
from jax.sharding import PartitionSpec as P

PANEL = 512
HALF = 256
STRIPE = 64
SUB = 8
LEAD = 3
BLOCK = 128
DEPTH = 256
SEGMENT = 256
VMEM = pl.BlockSpec(memory_space=pltpu.VMEM)
SMEM = pl.BlockSpec(memory_space=pltpu.SMEM)
ANYWHERE = pl.BlockSpec(memory_space=pl.ANY)


def call(kernel, out_shape, in_specs, microseconds, name, scratch=(), vmem=16):
    shapes = [jax.ShapeDtypeStruct(shape, dtype) for shape, dtype in out_shape]
    return pl.pallas_call(
        kernel,
        out_shape=shapes,
        in_specs=in_specs,
        out_specs=[VMEM] * len(shapes),
        scratch_shapes=list(scratch),
        compiler_params=pltpu.CompilerParams(vmem_limit_bytes=vmem * 1024 * 1024),
        cost_estimate=pl.CostEstimate(
            flops=int(microseconds * 1_100_000_000), bytes_accessed=1_000_000, transcendentals=0
        ),
        name=name,
    )


def join(parts, axis):
    return parts[0] if len(parts) == 1 else jnp.concatenate(parts, axis)


def shifted(value, amount):
    return lax.shift_right_logical(value, jnp.full_like(value, amount))


def sign_tile(seed_word, coordinate, feature, shape):
    rows = (lax.broadcasted_iota(jnp.int32, (shape[0], 1), 0) + coordinate) * jnp.int32(-1640531535)
    columns = (lax.broadcasted_iota(jnp.int32, (1, shape[1]), 1) + feature) * jnp.int32(668265263) + seed_word
    hashed = rows + columns
    hashed = (hashed ^ shifted(hashed, 16)) * jnp.int32(-2048144789)
    hashed = (hashed ^ shifted(hashed, 13)) * jnp.int32(-1028477387)
    decided = (hashed ^ shifted(hashed, 16)).astype(jnp.int16) & jnp.int16(128)
    return jnp.where(decided == 0, jnp.bfloat16(1.0), jnp.bfloat16(-1.0))


def segment_signs(seed_ref, coordinates, feature, width, index):
    first = lax.axis_index("tp") * coordinates + index * SEGMENT
    seed = seed_ref[0] if len(seed_ref.shape) == 1 else seed_ref[...]
    return sign_tile(seed, first, feature, (SEGMENT, width))


def project_step(seed_ref, chosen_ref, feature, width, index, total):
    start = pl.multiple_of(index * SEGMENT, SEGMENT)
    signs = segment_signs(seed_ref, chosen_ref.shape[1], feature, width, index)
    return total + jnp.dot(chosen_ref[:, pl.ds(start, SEGMENT)], signs, preferred_element_type=jnp.float32)


def project_tile(seed_ref, chosen_ref, feature, width, unroll):
    rows, coordinates = chosen_ref.shape
    step = functools.partial(project_step, seed_ref, chosen_ref, feature, width)
    zero = jnp.zeros((rows, width), jnp.float32)
    return lax.fori_loop(0, coordinates // SEGMENT, step, zero, unroll=unroll)


def even_of_pair():
    return lax.axis_index("tp") % 2 == 0


def panel_signs_kernel(seed_ref, signs_ref):
    coordinates, width = signs_ref.shape
    for step in range(coordinates // SEGMENT):
        signs_ref[step * SEGMENT : (step + 1) * SEGMENT, :] = segment_signs(
            seed_ref, coordinates, 0, width, step
        )


def panel_signs(seed, coordinates):
    return call(
        panel_signs_kernel, [((coordinates, PANEL), jnp.bfloat16)], [SMEM], 2, "panel_signs"
    )(seed)[0]


def panel_part_kernel(selection_ref, pool_ref, signs_ref, mine_ref, theirs_ref, chosen_ref):
    half = mine_ref.shape[0]
    shape = (pool_ref.shape[0], chosen_ref.shape[0])
    picked = jnp.where(lax.broadcasted_iota(jnp.int32, shape, 0) == selection_ref[...], 1.0, 0.0)
    chosen = tdot(picked.astype(jnp.bfloat16), pool_ref[...]).astype(jnp.bfloat16)
    chosen_ref[...] = chosen
    total = jnp.dot(chosen, signs_ref[...], preferred_element_type=jnp.float32)
    even = even_of_pair()
    mine_ref[...] = jnp.where(even, total[:half], total[half:])
    theirs_ref[...] = jnp.where(even, total[half:], total[:half])


def panel_part(seed, selection, pool):
    rows, coordinates = selection.shape[0], pool.shape[1]
    return call(
        panel_part_kernel,
        [((rows // 2, PANEL), jnp.float32)] * 2 + [((rows, coordinates), jnp.bfloat16)],
        [VMEM, VMEM, VMEM],
        1,
        "panel_part",
    )(selection[None, :], pool, panel_signs(seed.reshape(-1), coordinates))


def blocks_part_kernel(blocks, seed_ref, chosen_ref, _, *part_refs):
    width = part_refs[0].shape[1]
    for block, part_ref in zip(blocks, part_refs):
        part_ref[...] = project_tile(seed_ref, chosen_ref, block * width, width, len(blocks) <= 2)


def blocks_part(seed, chosen, blocks, width, after):
    return call(
        functools.partial(blocks_part_kernel, blocks),
        [((chosen.shape[0], width), jnp.float32)] * len(blocks),
        [VMEM, VMEM, ANYWHERE],
        2 * len(blocks),
        "blocks_part",
        vmem=32 if len(blocks) > 2 else 16,
    )(seed, chosen, after)


def other_parts_kernel(tp_count, blk_count, seed_ref, chosen_ref, _, *refs):
    *first_refs, mine_ref, theirs_ref = refs
    rows = chosen_ref.shape[0]
    half = rows // 2
    width = first_refs[0].shape[1]
    groups = width // HALF
    row_lanes = tp_count * groups // blk_count * HALF
    even = even_of_pair()
    for ref in (mine_ref, theirs_ref):
        ref[:, : row_lanes + 2 * width] = jnp.zeros((half, row_lanes + 2 * width), jnp.float32)

    def place(ref, lane, part):
        ref[:, lane : lane + width] = part[:half]
        ref[:, lane + width : lane + 2 * width] = part[half:]

    for block in range(1, tp_count):
        lane = row_lanes + block // 2 * 2 * width
        if block <= len(first_refs):
            part = first_refs[block - 1][...]
        else:
            part = project_tile(seed_ref, chosen_ref, block * width, width, tp_count <= 4)
        own = lax.axis_index("tp") % 2 == block % 2
        pl.when(own)(functools.partial(place, mine_ref, lane, part))
        pl.when(jnp.logical_not(own))(functools.partial(place, theirs_ref, lane, part))
        for which in range(groups):
            group = block * groups + which

            @pl.when(lax.axis_index("blk") == group % blk_count)
            def _(part=part[:, which * HALF : (which + 1) * HALF], lane=group // blk_count * HALF):
                mine_ref[:, lane : lane + HALF] = jnp.where(even, part[:half], part[half:])
                theirs_ref[:, lane : lane + HALF] = jnp.where(even, part[half:], part[:half])


def other_parts(seed, chosen, first, tp_count, blk_count, after):
    rows, width = first[0].shape
    lanes = tp_count * (width // HALF) // blk_count * HALF + tp_count // 2 * 2 * width
    return call(
        functools.partial(other_parts_kernel, tp_count, blk_count),
        [((rows // 2, lanes), jnp.float32)] * 2,
        [VMEM, VMEM, ANYWHERE] + [VMEM] * len(first),
        2 * (tp_count - 1 - len(first)),
        "other_parts",
        vmem=16 if tp_count <= 4 else 48,
    )(seed, chosen, after, *first)


def group_at(rows, index, count):
    found = rows[:, :HALF]
    for place in range(1, count):
        found = jnp.where(index == place, rows[:, place * HALF : (place + 1) * HALF], found)
    return found


def halve_kernel(ex_count, bit, left_ref, right_ref, keep_ref, send_ref):
    row_lanes = ex_count * HALF
    upper = lax.axis_index("tp") & bit != 0
    total = left_ref[...] + right_ref[...]
    middle = (total.shape[1] + row_lanes) // 2
    keep_ref[:, :row_lanes] = total[:, :row_lanes]
    send_ref[:, :row_lanes] = total[:, :row_lanes]
    keep_ref[:, row_lanes:] = jnp.where(upper, total[:, middle:], total[:, row_lanes:middle])
    send_ref[:, row_lanes:] = jnp.where(upper, total[:, row_lanes:middle], total[:, middle:])


def halve(left, right, ex_count, bit):
    shape = (left.shape[0], (left.shape[1] + ex_count * HALF) // 2)
    return call(
        functools.partial(halve_kernel, ex_count, bit),
        [(shape, jnp.float32)] * 2,
        [VMEM, VMEM],
        0.5,
        "halve",
    )(left, right)


def last_half(ex_count, holder, left_ref, right_ref):
    def picked(index, places):
        found = None
        for place, lanes in enumerate(places):
            value = (left_ref[:, lanes], right_ref[:, lanes])
            if found is None:
                found = value
            else:
                found = tuple(jnp.where(index == place, new, old) for new, old in zip(value, found))
        return found[0] + found[1]

    groups = [slice(place * HALF, (place + 1) * HALF) for place in range(ex_count)]
    row_lanes = ex_count * HALF
    middle = (left_ref.shape[1] + row_lanes) // 2
    blocks = [slice(row_lanes, middle), slice(middle, left_ref.shape[1])]
    rows = [picked(holder ^ step, groups) for step in range(1, ex_count)]
    return rows, picked(holder & 1, blocks)


def send_kernel(ex_count, left_ref, right_ref, send_ref):
    rows, columns = last_half(ex_count, lax.axis_index("tp") // 2 ^ 1, left_ref, right_ref)
    lanes = (ex_count - 1) * HALF
    send_ref[:, :lanes] = join(rows, 1)
    send_ref[:, lanes:] = columns


def last_sent(left, right, ex_count):
    row_lanes = ex_count * HALF
    shape = (left.shape[0], (left.shape[1] - row_lanes) // 2 + row_lanes - HALF)
    return call(
        functools.partial(send_kernel, ex_count),
        [(shape, jnp.float32)],
        [VMEM, VMEM],
        0.5,
        "last_sent",
    )(left, right)[0]


def pieces_kernel(ex_count, scaling, left_ref, right_ref, came_ref, _, *piece_refs):
    holder = lax.axis_index("tp") // 2
    rows, columns = last_half(ex_count, holder, left_ref, right_ref)
    rows = [
        ((row + came_ref[:, place * HALF : (place + 1) * HALF]) * scaling).astype(jnp.bfloat16)
        for place, row in enumerate(rows)
    ]
    columns = ((columns + came_ref[:, (ex_count - 1) * HALF :]) * scaling).astype(jnp.bfloat16)
    for step, ref in enumerate(piece_refs):
        distance = lax.axis_index("ex") ^ step ^ holder
        wanted = rows[0]
        for place in range(1, ex_count - 1):
            wanted = jnp.where(distance - 1 == place, rows[place], wanted)
        ref[:, :HALF] = wanted
        ref[:, HALF:] = columns


def pieces(left, right, came, ex_count, scaling, after):
    shape = (left.shape[0], came.shape[1] - (ex_count - 2) * HALF)
    return call(
        functools.partial(pieces_kernel, ex_count, scaling),
        [(shape, jnp.bfloat16)] * ex_count,
        [VMEM, VMEM, VMEM, ANYWHERE],
        0.5,
        "pieces",
    )(left, right, came, after)


def tdot(left, right):
    return lax.dot_general(left, right, (((0,), (0,)), ((), ())), preferred_element_type=jnp.float32)


def row_of(value, row):
    return jnp.broadcast_to(value[row : row + 1, :], value.shape)


def factor_stripe(rows_u, rows_z, offset):
    groups = len(rows_u)
    count = 8 * groups
    sub = lax.broadcasted_iota(jnp.int32, (8, BLOCK), 0)
    rows_u, rows_z = list(rows_u), list(rows_z)
    pivots = [jnp.ones((8, BLOCK), jnp.float32) for _ in range(groups)]

    def taken(base):
        return {
            c: {
                v: jnp.broadcast_to(rows_u[v][:, offset + c : offset + c + 1], (8, BLOCK))
                for v in range(c // 8, groups)
            }
            for c in range(base, base + SUB)
        }

    columns = taken(0)
    pivot = row_of(columns[0][0], 0)
    for j in range(count):
        g, s = divmod(j, 8)
        if j % SUB == SUB - LEAD and j + LEAD < count:
            columns.update(taken(j + LEAD))
        column = columns.pop(j)
        inverse = 1.0 / pivot
        pivots[g] = jnp.where(sub == s, pivot, pivots[g])
        if j + 1 < count:
            n, r = divmod(j + 1, 8)
            weight = row_of(column[n], r)
            following = columns[j + 1]
            pivot = row_of(following[n], r) - (weight * weight) * inverse
            for v in range(n, groups):
                following[v] = following[v] - (column[v] * weight) * inverse
        factors = {v: column[v] * inverse for v in range(g, groups)}
        for c, other in columns.items():
            if c > j + 1:
                weight = row_of(column[c // 8], c % 8)
                for v in range(c // 8, groups):
                    other[v] = other[v] - factors[v] * weight
        factors[g] = jnp.where(sub > s, factors[g], 0.0)
        row_u, row_z = row_of(rows_u[g], s), row_of(rows_z[g], s)
        for v in range(g + (s == 7), groups):
            rows_u[v] = rows_u[v] - factors[v] * row_u
            rows_z[v] = rows_z[v] - factors[v] * row_z
    scales = [lax.rsqrt(pivot) for pivot in pivots]
    return (
        [row * scale for row, scale in zip(rows_u, scales)],
        [row * scale for row, scale in zip(rows_z, scales)],
    )


def thirds(value):
    high = value.astype(jnp.bfloat16)
    rest = value - high.astype(jnp.float32)
    middle = rest.astype(jnp.bfloat16)
    return high, middle, (rest - middle.astype(jnp.float32)).astype(jnp.bfloat16)


def exact_dot(left, right, axes=(1, 0)):
    left_parts, right_parts = thirds(left), thirds(right)
    terms = ((0, 0), (0, 1), (1, 0), (0, 2), (2, 0), (1, 1))
    count = max(1, min(len(terms), DEPTH // left.shape[axes[0]]))
    total = None
    for start in range(0, len(terms), count):
        some = terms[start : start + count]
        term = lax.dot_general(
            join([left_parts[i] for i, _ in some], axes[0]),
            join([right_parts[j] for _, j in some], axes[1]),
            (((axes[0],), (axes[1],)), ((), ())),
            preferred_element_type=jnp.float32,
        )
        total = term if total is None else total + term
    return total


def identity_mask(shape):
    return lax.broadcasted_iota(jnp.int32, shape, 0) == lax.broadcasted_iota(jnp.int32, shape, 1)


def factor_start(block):
    unit = identity_mask(block.shape).astype(jnp.float32)
    return factor_step(block, unit, 0)


def factor_step(rest_u, rest_z, offset):
    groups = STRIPE // 8
    upper, inverse = factor_stripe(
        [rest_u[8 * v : 8 * v + 8] for v in range(groups)],
        [rest_z[8 * v : 8 * v + 8] for v in range(groups)],
        offset,
    )
    upper, inverse = jnp.concatenate(upper, axis=0), jnp.concatenate(inverse, axis=0)
    if offset + STRIPE == BLOCK:
        return inverse, None, None
    update = exact_dot(upper, jnp.concatenate([upper, inverse], axis=1), (0, 0))[offset + STRIPE :]
    return inverse, rest_u[STRIPE:] - update[:, :BLOCK], rest_z[STRIPE:] - update[:, BLOCK:]


def factor_end(inverse, rest_u, rest_z):
    done = [inverse]
    for offset in range(STRIPE, BLOCK, STRIPE):
        inverse, rest_u, rest_z = factor_step(rest_u, rest_z, offset)
        done.append(inverse)
    return jnp.concatenate(done, axis=0)


def in_pair_order(even, refs, lanes=slice(None)):
    values = [ref[:, lanes] for ref in refs]
    count = len(values) // 2
    mine, other = join(values[:count], 0), join(values[count:], 0)
    return join([jnp.where(even, mine, other), jnp.where(even, other, mine)], 0)


def eliminate(gram, turned, upper_refs, done_refs, rest_refs, started=None):
    square = (BLOCK, BLOCK)
    keep = lax.broadcasted_iota(jnp.int32, square, 0) <= lax.broadcasted_iota(jnp.int32, square, 1)
    block = gram[:BLOCK, :BLOCK]
    for index, (upper_ref, done_ref) in enumerate(zip(upper_refs, done_refs)):
        if index > 0 or started is None:
            started = factor_start(block)
        inverse = factor_end(*started)
        if index + 1 < len(upper_refs):
            beside = exact_dot(inverse, gram[:BLOCK, BLOCK : 2 * BLOCK])
            ahead = gram[BLOCK : 2 * BLOCK, BLOCK : 2 * BLOCK] - exact_dot(beside, beside, (0, 0))
        upper_ref[:, :BLOCK] = jnp.where(keep, exact_dot(inverse, block), 0.0)
        done = exact_dot(turned[:, :BLOCK], inverse, (1, 1))
        done_ref[...] = done
        if gram.shape[0] > BLOCK:
            rest = exact_dot(inverse, gram[:BLOCK, BLOCK:])
            upper_ref[:, BLOCK:] = rest
            gram = gram[BLOCK:, BLOCK:] - exact_dot(rest, rest, (0, 0))
            turned = turned[:, BLOCK:] - exact_dot(done, rest)
        if index + 1 < len(upper_refs):
            block = ahead
    if rest_refs:
        rest_refs[0][...] = gram
        rest_refs[1][...] = turned


def first_blocks_kernel(blocks, count, ridge_ref, *refs):
    phi_refs, out_refs = refs[:count], refs[count:]
    phi = in_pair_order(even_of_pair(), phi_refs)
    examples, width = phi.shape
    gram = tdot(phi, phi) * (1.0 / examples) + jnp.where(identity_mask((width, width)), ridge_ref[...], 0.0)
    eliminate(
        gram, phi.astype(jnp.float32), out_refs[:blocks], out_refs[blocks : 2 * blocks], out_refs[2 * blocks :]
    )


def start_block_kernel(block_ref, *out_refs):
    for ref, value in zip(out_refs, factor_start(block_ref[:BLOCK, :BLOCK])):
        ref[...] = value


def last_blocks_kernel(blocks, gram_ref, turned_ref, inverse_ref, rest_u_ref, rest_z_ref, *refs):
    started = (inverse_ref[...], rest_u_ref[...], rest_z_ref[...])
    eliminate(gram_ref[...], turned_ref[...], refs[:blocks], refs[blocks:], (), started)


def block_shapes(width, examples, blocks):
    rest = width - blocks * BLOCK
    shapes = [(BLOCK, width - index * BLOCK) for index in range(blocks)] + [(examples, BLOCK)] * blocks
    if rest:
        shapes += [(rest, rest), (examples, rest)]
    return [(shape, jnp.float32) for shape in shapes]


def taken_apart(results, blocks):
    return list(results[:blocks]), list(results[blocks : 2 * blocks]), results[2 * blocks :]


def first_blocks(ridge, phi, blocks):
    examples, width = sum(part.shape[0] for part in phi), phi[0].shape[1]
    results = call(
        functools.partial(first_blocks_kernel, blocks, len(phi)),
        block_shapes(width, examples, blocks),
        [VMEM] * (1 + len(phi)),
        3.5,
        "gram_first_blocks",
    )(ridge, *phi)
    return taken_apart(results, blocks)


def start_block(gram):
    shapes = [(STRIPE, BLOCK), (BLOCK - STRIPE, BLOCK), (BLOCK - STRIPE, BLOCK)]
    return call(
        start_block_kernel, [(shape, jnp.float32) for shape in shapes], [VMEM], 1.5, "start_block"
    )(gram)


def last_blocks(rest, started):
    gram, turned = rest
    blocks = gram.shape[0] // BLOCK
    results = call(
        functools.partial(last_blocks_kernel, blocks),
        block_shapes(gram.shape[0], turned.shape[0], blocks),
        [VMEM] * (2 + len(started)),
        4.5,
        "last_blocks",
    )(gram, turned, *started)
    return taken_apart(results, blocks)


def assembled_columns(refs, height, width):
    return join([ref[:, start : start + width] for start in (height, height + width) for ref in refs], 0)


def lower(uppers, row, lane):
    if row < lane:
        return jnp.zeros((BLOCK, BLOCK), jnp.float32)
    return uppers[lane // BLOCK][:, row - lane : row - lane + BLOCK].T


def put_lower(uppers, ref, first):
    for row in range(0, ref.shape[0], BLOCK):
        for lane in range(0, ref.shape[1], BLOCK):
            ref[row : row + BLOCK, lane : lane + BLOCK] = lower(uppers, first + row, lane)


def solve(features, parts_ref):
    turned = features.T
    product = jnp.dot(join([turned] * 3, 1), parts_ref[...], preferred_element_type=jnp.float32)
    return turned, product * (1.0 / features.shape[0])


def column_kernel(blocks, count, height, *refs):
    uppers, dones = refs[:blocks], refs[blocks : 2 * blocks]
    phi_refs, mine = refs[2 * blocks : 2 * blocks + count], refs[2 * blocks + count : -6]
    columns_ref, parts_ref, *third_refs, solved_ref = refs[-6:]
    width = columns_ref.shape[1]
    column_block = lax.axis_index("tp")
    phi = in_pair_order(even_of_pair(), phi_refs)
    columns = jnp.where(column_block == 0, phi, assembled_columns(mine, height, width))
    columns_ref[...] = columns
    parts_ref[...] = join(list(thirds(join([ref[...] for ref in dones], 1))), 0)
    solved_ref[...] = solve(columns, parts_ref)[1]
    pl.when(column_block == 0)(functools.partial(put_lower, uppers, solved_ref, 0))
    for ref, part in zip(third_refs, thirds(solved_ref[...])):
        ref[...] = part


def columns_solved(uppers, dones, phi, mine, height, width):
    panel, examples = uppers[0].shape[1], sum(part.shape[0] for part in phi)
    operands = [*uppers, *dones, *phi, *mine]
    shapes = [(examples, width), (3 * examples, panel)] + [(width, panel)] * 3
    return call(
        functools.partial(column_kernel, len(uppers), len(phi), height),
        [(shape, jnp.bfloat16) for shape in shapes],
        [VMEM] * len(operands),
        1,
        "columns_solved",
        [pltpu.VMEM((width, panel), jnp.float32)],
        vmem=24,
    )(*operands)


def finish_kernel(blocks, count, blk_count, ridge_ref, columns_ref, parts_ref, *refs):
    solved, refs = [ref[...] for ref in refs[:3]], refs[3:]
    uppers = refs[:blocks]
    phi_refs, piece_refs = refs[blocks : blocks + count], refs[blocks + count : -2]
    panel_ref, trailing_ref = refs[-2:]
    height, panel = panel_ref.shape
    width = trailing_ref.shape[1]
    even = even_of_pair()
    ex_index, column_block, blk_index = (lax.axis_index(axis) for axis in ("ex", "tp", "blk"))
    row_group = ex_index * blk_count + blk_index
    phi = in_pair_order(even, phi_refs)
    rows = in_pair_order(even, piece_refs, slice(0, height))
    columns = columns_ref[...]
    pair_columns = assembled_columns(piece_refs[count // 2 :], height, width)
    groups = width // height
    held = jnp.where(blk_index // groups == column_block % 2, columns, pair_columns)
    for place in range(groups):
        inside = (ex_index == column_block // 2) & (blk_index % groups == place)
        rows = jnp.where(inside, held[:, place * height : (place + 1) * height], rows)
    for start in range(0, panel, height):
        rows = jnp.where(row_group * height == start, phi[:, start : start + height], rows)
    turned, panel_ref[...] = solve(rows, parts_ref)
    for group in range(panel // height):
        pl.when(row_group == group)(functools.partial(put_lower, uppers, panel_ref, group * height))
    shape = (height, width)
    diagonal = row_group * height + lax.broadcasted_iota(
        jnp.int32, shape, 0
    ) == column_block * width + lax.broadcasted_iota(jnp.int32, shape, 1)
    gram = jnp.dot(turned, columns, preferred_element_type=jnp.float32) * (1.0 / columns.shape[0])
    total = gram + jnp.where(diagonal, ridge_ref[...], 0.0)
    for left, right in zip(*term_parts(thirds(panel_ref[...]), solved)):
        total = total - lax.dot_general(
            left, right, (((1,), (1,)), ((), ())), preferred_element_type=jnp.float32
        )
    trailing_ref[...] = total


def term_parts(left_parts, right_parts):
    terms = ((0, 0), (0, 1), (1, 0), (0, 2), (2, 0), (1, 1))
    return [left_parts[i] for i, _ in terms], [right_parts[j] for _, j in terms]


def finish(ridge, uppers, dones, phi, gathered, height, width, blk_count):
    panel = uppers[0].shape[1]
    mine = gathered[: len(gathered) // 2]
    solved = columns_solved(uppers, dones, phi, mine, height, width)
    operands = [*solved, *uppers, *phi, *gathered]
    return call(
        functools.partial(finish_kernel, len(uppers), len(phi), blk_count),
        [((height, panel), jnp.float32), ((height, width), jnp.float32)],
        [VMEM] * (1 + len(operands)),
        2,
        "finish",
        vmem=24,
    )(ridge, *operands)


def swapped(value, axis, bit):
    return lax.ppermute(value, axis, [(s, s ^ bit) for s in range(lax.axis_size(axis))])


def ex_parts(own):
    return [own[0]] + [swapped(own[step], "ex", step) for step in range(1, lax.axis_size("ex"))]


def with_pair(parts):
    return list(parts) + [swapped(part, "tp", 1) for part in parts]


def shards(gradients, selection, seed_value, ridge_value):
    ex_count = lax.axis_size("ex")
    tp_count = lax.axis_size("tp")
    blk_count = lax.axis_size("blk")
    coord_dev = gradients.shape[1]
    column_width = HALF * ex_count * blk_count // tp_count
    scaling = 1.0 / math.sqrt(coord_dev * tp_count)
    seed, ridge = seed_value.reshape(1, 1), ridge_value.reshape(1, 1)

    mine, theirs, chosen = panel_part(seed, selection, gradients)
    total = mine + swapped(theirs, "tp", 1)
    halves = total
    bit = 2
    while bit < tp_count:
        total = total + swapped(total, "tp", bit)
        bit *= 2
    phi = ex_parts([(total * scaling).astype(jnp.bfloat16)] * ex_count)

    first = blocks_part(seed, chosen, range(1, 1 + tp_count // 2), column_width, halves)
    left, right = other_parts(seed, chosen, first, tp_count, blk_count, total)
    phi[1:], right = lax.optimization_barrier((phi[1:], right))
    right = swapped(right, "tp", 1)
    bit = tp_count // 2
    while bit > 2:
        left, right = halve(left, right, ex_count, bit)
        right = swapped(right, "tp", bit)
        bit //= 2
    came = swapped(last_sent(left, right, ex_count), "tp", 2)

    phi = with_pair(phi)
    half = PANEL // BLOCK // 2
    uppers, dones, rest = first_blocks(ridge, phi, half)
    started = start_block(rest[0])
    gathered = pieces(left, right, came, ex_count, scaling, started[0])
    other = swapped(gathered[0], "tp", 1)
    gathered = ex_parts(gathered)
    started, other = lax.optimization_barrier((started, other))
    more_uppers, more_dones, _ = last_blocks(rest, started)
    gathered[1:], more_dones = lax.optimization_barrier((gathered[1:], more_dones))
    gathered = [*gathered, other, *(swapped(part, "tp", 1) for part in gathered[1:])]
    uppers, dones = uppers + more_uppers, dones + more_dones
    return tuple(finish(ridge, uppers, dones, phi, gathered, HALF, column_width, blk_count))


def solution(mesh):
    in_specs = (P("ex", "tp"), P("ex"), P(), P())
    out_specs = (P(("ex", "blk"), None), P(("ex", "blk"), "tp"))
    return jax.shard_map(shards, mesh=mesh, in_specs=in_specs, out_specs=out_specs, check_vma=False)
```
